256 devices in a mesh: gx: 8 (over y, core), gy: 4 (over x), gz: 8 (over z).
Axes of the slice: x: 4, y: 4, z: 8, core: 2. Of those that a mesh axis runs over, the one named last changes fastest.
Arguments:
- fine_old: float32 [1536, 5, 4096], P(('gx', 'gy', 'gz'))
- send_left: int32 [512], P(('gx', 'gy', 'gz')), may hold values from 0 to 5, as said below
- send_right: int32 [512], P(('gx', 'gy', 'gz')), may hold values from 0 to 5
- new_source: int32 [1536], P(('gx', 'gy', 'gz')), may hold values from 0 to 11, as said below
- face_source: int32 [1536, 6], P(('gx', 'gy', 'gz')), may hold values from 0 to 113, as said below
- request_slot: int32 [3584], P(('gx', 'gy', 'gz')), may hold values from 0 to 127, as said below
- request_code: int32 [3584], P(('gx', 'gy', 'gz')), may hold values from 0 to 223, as said below
- coarse_old: float32 [1024, 5, 4096], P(('gx', 'gy', 'gz'))
- coarse_new: float32 [1024, 5, 4096], P(('gx', 'gy', 'gz'))
- coarse_flux: float32 [1024, 6, 5, 256], P(('gx', 'gy', 'gz')), may hold values from -8 to 8
Outputs:
- fine_state: float32 [1536, 5, 4096], P(('gx', 'gy', 'gz'))
- coarse_state: float32 [1024, 5, 4096], P(('gx', 'gy', 'gz'))
The draws below stay inside these ranges and needn't reach their ends.
Inputs may be any that keep to these rules, and one draw needn't show every extreme that they name: Distinct old slots of one device, none listed in both send_left and send_right. `new_source`: indices into the pool: 6 own old blocks, 2 from the device before, 2 from the device after, then 2 created blocks; no index repeats on a device, every created block is used, and none names a device beyond the ends of the curve. `face_source`: an entry e below 108 names face e % 6, the face opposite, of block e // 6 of the devices before, at and after this one, never beyond the curve's ends; at most 3 entries of a device name the device before and at most 3 the device after, and every device away from the curve's ends has exactly 3 of each; 108 + r names request r, each r below 6 exactly once on a device. `request_slot`: distinct on one device, so at most 4 requests of one device reach one peer; in every draw one peer of each gx group receives 4 from every device of the group. `request_code`: the first 6 of a device are below 96; the last 8 are not, the 4 pieces of one created block in order and to one peer.
All inputs are finite; a program needn't handle non-finite values.
Results may differ from the reference program's by a relative error of at most 0.0003.
Values sent between devices are 32-bit elements; how exact they have to be, the bound alone decides.
A program may use at most 128 MiB of HBM per device.

```python
import jax
import jax.numpy as jnp
from jax import lax

BS = 16
HALF = 8
CELLS = 4096
PATCH = 128
OCTP = 4
SLOTS = 6
CSLOTS = 4
MOVE = 2
NEWB = 2
CAP = 4
PEERS = 32
RANKS = 256
SIDE = 3
FACEREQ = 6
REQ = 14
NBLK = 1536
NCBLK = 1024


heat_ratio = 1.4


def gas_state(key, row_count, exponent, offset):
    subkeys = jax.random.split(key, 3)
    grid_shape = (row_count, BS * BS * BS)
    density = 0.5 * 4.0 ** jax.random.uniform(subkeys[0], grid_shape) ** exponent
    pressure = 0.5 * 4.0 ** jax.random.uniform(subkeys[1], grid_shape) ** exponent
    velocity = jax.random.uniform(subkeys[2], (3,) + grid_shape, minval=-0.5, maxval=0.5)
    velocity = jnp.clip(velocity + offset, -0.5, 0.5)
    momenta = density[None] * velocity
    energy = pressure / (heat_ratio - 1.0) + 0.5 * density * jnp.sum(velocity * velocity, axis=0)
    return jnp.stack([density, momenta[0], momenta[1], momenta[2], energy], axis=1).astype(jnp.float32)


def device_plan(key, device_idx):
    local = jax.random.fold_in(jax.random.fold_in(key, 2), device_idx)
    subkeys = jax.random.split(local, 13)
    shuffled = jax.random.permutation(subkeys[0], SLOTS).astype(jnp.int32)
    to_left = shuffled[:MOVE]
    to_right = shuffled[MOVE:2 * MOVE]
    spare = shuffled[2 * MOVE:]
    use_left = jax.random.randint(subkeys[1], (), 1, MOVE + 1)
    use_right = jax.random.randint(subkeys[2], (), 1, MOVE + 1)
    first_dev = device_idx == 0
    last_dev = device_idx == RANKS - 1
    use_left = jnp.where(first_dev, 0, jnp.where(last_dev | (device_idx == 1), MOVE, use_left))
    use_right = jnp.where(last_dev, 0, jnp.where(first_dev, MOVE, use_right))
    positions = jnp.arange(SLOTS, dtype=jnp.int32)
    mark_a = use_left
    mark_b = mark_a + use_right
    mark_c = mark_b + NEWB
    spare_pos = jnp.clip(positions - mark_c, 0, SLOTS - 2 * MOVE - 1)
    source = jnp.where(positions < mark_a, SLOTS + positions, jnp.where(positions < mark_b, SLOTS + MOVE + positions - mark_a, jnp.where(positions < mark_c, SLOTS + 2 * MOVE + positions - mark_b, spare[spare_pos])))
    source = source[jax.random.permutation(subkeys[3], SLOTS)].astype(jnp.int32)
    face_total = 6 * SLOTS
    face_ids = jnp.arange(face_total, dtype=jnp.int32)
    scores = jax.random.randint(subkeys[4], (face_total,), 0, 2 ** 20) * face_total + face_ids
    by_score = jnp.argsort(scores).astype(jnp.int32)
    ranking = jnp.argsort(by_score).astype(jnp.int32)
    face_dir = face_ids % 6
    opposite = face_dir + 1 - 2 * (face_dir % 2)
    own_pick = SLOTS + jax.random.randint(subkeys[5], (face_total,), 0, SLOTS)
    side_block = jax.random.randint(subkeys[12], (face_total,), 0, SLOTS)
    left_set = (ranking >= FACEREQ) & (ranking < FACEREQ + SIDE) & jnp.logical_not(first_dev)
    right_set = (ranking >= FACEREQ + SIDE) & (ranking < FACEREQ + 2 * SIDE) & jnp.logical_not(last_dev)
    neighbour = jnp.where(left_set, side_block, jnp.where(right_set, 2 * SLOTS + side_block, own_pick))
    face_source = jnp.where(ranking < FACEREQ, 18 * SLOTS + ranking, neighbour * 6 + opposite).astype(jnp.int32)
    req_dir = opposite[by_score[:FACEREQ]]
    face_block = jax.random.randint(subkeys[6], (FACEREQ,), 0, CSLOTS)
    face_quad = jax.random.randint(subkeys[7], (FACEREQ,), 0, 4)
    face_codes = (face_block * 6 + req_dir) * 4 + face_quad
    oct_block = jax.random.randint(subkeys[8], (NEWB,), 0, CSLOTS)
    oct_which = jax.random.randint(subkeys[9], (NEWB,), 0, 8)
    oct_codes = 24 * CSLOTS + ((oct_block * 8 + oct_which)[:, None] * OCTP + jnp.arange(OCTP, dtype=jnp.int32)[None, :]).reshape(-1)
    group_idx = device_idx // PEERS
    busy_peer = jax.random.randint(jax.random.fold_in(jax.random.fold_in(key, 3), group_idx), (), 0, PEERS)
    peer_ids = jnp.arange(PEERS, dtype=jnp.int32)
    peer_scores = jax.random.randint(subkeys[10], (PEERS,), 0, 2 ** 20) * PEERS + peer_ids
    peer_scores = jnp.where(peer_ids == busy_peer, -1, peer_scores)
    peer_order = jnp.argsort(peer_scores).astype(jnp.int32)
    barred = jnp.zeros((PEERS,), bool).at[peer_order[:1 + NEWB]].set(True)
    slot_ids = jnp.arange(PEERS * CAP, dtype=jnp.int32)
    slot_scores = jax.random.randint(subkeys[11], (PEERS * CAP,), 0, 2 ** 20) * (PEERS * CAP) + slot_ids
    slot_scores = jnp.where(barred[slot_ids // CAP], 2 ** 30 + slot_ids, slot_scores)
    chosen = jnp.argsort(slot_scores)[:FACEREQ - CAP].astype(jnp.int32)
    face_slots = jnp.concatenate([busy_peer * CAP + jnp.arange(CAP, dtype=jnp.int32), chosen])
    oct_slots = (peer_order[1:1 + NEWB][:, None] * CAP + jnp.arange(OCTP, dtype=jnp.int32)[None, :]).reshape(-1)
    slots_all = jnp.concatenate([face_slots, oct_slots]).astype(jnp.int32)
    codes_all = jnp.concatenate([face_codes, oct_codes]).astype(jnp.int32)
    return (to_left, to_right, source, face_source, slots_all, codes_all)


def plan(key):
    outs = jax.vmap(device_plan, in_axes=(None, 0))(key, jnp.arange(RANKS, dtype=jnp.int32))
    return (outs[0].reshape(-1), outs[1].reshape(-1), outs[2].reshape(-1), outs[3].reshape(RANKS * SLOTS, 6), outs[4].reshape(-1), outs[5].reshape(-1))


def draw_send_left(key, part):
    return plan(key)[0]


def draw_send_right(key, part):
    return plan(key)[1]


def draw_new_source(key, part):
    return plan(key)[2]


def draw_face_source(key, part):
    return plan(key)[3]


def draw_request_slot(key, part):
    return plan(key)[4]


def draw_request_code(key, part):
    return plan(key)[5]


def draw_fine_old(key, part):
    key = jax.random.fold_in(key, 21)
    return gas_state(key, NBLK, 1.0, 0.0)


def draw_coarse_old(key, part):
    key = jax.random.fold_in(key, 22)
    return gas_state(key, NCBLK, 1.0, 0.0)


def draw_coarse_new(key, part):
    key = jax.random.fold_in(key, 23)
    return gas_state(key, NCBLK, 1.0, 0.0)


def block_levels(stream_key, shape, cuts, low, high):
    loudness, own = 1.0, jax.random.fold_in(stream_key, 6)
    for axis_at, shards_of in cuts:
        steps = jnp.exp(jax.random.uniform(jax.random.fold_in(own, axis_at), (shards_of,), jnp.float32, low / len(cuts), high / len(cuts)))
        loudness = loudness * jnp.repeat(steps, shape[axis_at] // shards_of).reshape([-1 if axis == axis_at else 1 for axis in range(len(shape))])
    return loudness


def scatter_about(own_key, extent, spread, reach, cuts=(), held_as=jnp.bfloat16):
    factor_of = block_levels(own_key, extent, cuts, -0.22, 0.18) if cuts else 1.0
    entries = jax.random.normal(own_key, extent, jnp.float32) * spread * factor_of
    return jnp.minimum(jnp.maximum(entries, -reach), reach).astype(held_as)


def setup_inputs(seed: int = 0) -> dict:
    splits = jax.random.split(jax.random.key(seed), 11)
    return {
        "fine_old": draw_fine_old(jax.random.fold_in(splits[10], 71), 0),
        "send_left": draw_send_left(jax.random.fold_in(splits[10], 71), 0),
        "send_right": draw_send_right(jax.random.fold_in(splits[10], 71), 0),
        "new_source": draw_new_source(jax.random.fold_in(splits[10], 71), 0),
        "face_source": draw_face_source(jax.random.fold_in(splits[10], 71), 0),
        "request_slot": draw_request_slot(jax.random.fold_in(splits[10], 71), 0),
        "request_code": draw_request_code(jax.random.fold_in(splits[10], 71), 0),
        "coarse_old": draw_coarse_old(jax.random.fold_in(splits[10], 71), 0),
        "coarse_new": draw_coarse_new(jax.random.fold_in(splits[10], 71), 0),
        "coarse_flux": scatter_about(splits[9], (NCBLK, 6, 5, BS * BS), 2.0, 8.0, ((0, 256),), jnp.float32),
    }


heat_ratio = 1.4
courant = 0.08

def euler_flux(state, axis_idx):
    density = state[:, 0]
    momenta = state[:, 1:4]
    kinetic = 0.5 * lax.optimization_barrier(jnp.sum(momenta * momenta, axis=1)) / density
    pressure = (heat_ratio - 1.0) * (state[:, 4] - kinetic)
    velocity = state[:, 1 + axis_idx] / density
    face_flux = state * jnp.expand_dims(velocity, 1)
    face_flux = face_flux.at[:, 1 + axis_idx].add(pressure)
    face_flux = face_flux.at[:, 4].add(pressure * velocity)
    speeds = jnp.abs(velocity) + jnp.sqrt(heat_ratio * pressure / density)
    return (face_flux, speeds)

def boundary_layers(blocks):
    return jnp.stack([blocks[:, :, 0], blocks[:, :, -1], blocks[:, :, :, 0], blocks[:, :, :, -1], blocks[:, :, :, :, 0], blocks[:, :, :, :, -1]], axis=1)

def advance(blocks, ghosts):
    edge_len = blocks.shape[2]
    updated = blocks
    borders = []
    for axis_idx in range(3):
        along_dim = 2 + axis_idx
        low_ghost = jnp.expand_dims(ghosts[:, 2 * axis_idx], along_dim)
        high_ghost = jnp.expand_dims(ghosts[:, 2 * axis_idx + 1], along_dim)
        padded = jnp.concatenate([low_ghost, blocks, high_ghost], axis=along_dim)
        face_flux, speeds = euler_flux(padded, axis_idx)
        left_flux = lax.slice_in_dim(face_flux, 0, edge_len + 1, axis=along_dim)
        right_flux = lax.slice_in_dim(face_flux, 1, edge_len + 2, axis=along_dim)
        left_state = lax.slice_in_dim(padded, 0, edge_len + 1, axis=along_dim)
        right_state = lax.slice_in_dim(padded, 1, edge_len + 2, axis=along_dim)
        left_speed = lax.slice_in_dim(speeds, 0, edge_len + 1, axis=along_dim - 1)
        right_speed = lax.slice_in_dim(speeds, 1, edge_len + 2, axis=along_dim - 1)
        across = 0.5 * (left_flux + right_flux) - 0.5 * jnp.expand_dims(jnp.maximum(left_speed, right_speed), 1) * (right_state - left_state)
        change = lax.slice_in_dim(across, 1, edge_len + 1, axis=along_dim) - lax.slice_in_dim(across, 0, edge_len, axis=along_dim)
        updated = updated - courant * change
        borders.append(lax.index_in_dim(across, 0, axis=along_dim, keepdims=False))
        borders.append(lax.index_in_dim(across, edge_len, axis=along_dim, keepdims=False))
    return (updated, jnp.stack(borders, axis=1))

def make_payload(req_code, first_block, block_count, volume, old_faces, new_faces, pieces):
    half_len = volume.shape[2] // 2
    zero_idx = jnp.zeros((), jnp.int32)
    face_code = jnp.clip(req_code, 0, 24 * block_count - 1).astype(jnp.int32)
    block_idx = (first_block + face_code // 24).astype(jnp.int32)
    direction = face_code // 4 % 6
    quadrant = face_code % 4
    start = (block_idx, direction, zero_idx, (quadrant // 2 * half_len).astype(jnp.int32), (quadrant % 2 * half_len).astype(jnp.int32))
    old_part = lax.dynamic_slice(old_faces, start, (1, 1, 5, half_len, half_len)).reshape(5, half_len * half_len)
    new_part = lax.dynamic_slice(new_faces, start, (1, 1, 5, half_len, half_len)).reshape(5, half_len * half_len)
    face_part = jnp.concatenate([old_part, new_part], axis=1)
    oct_code = jnp.clip(req_code - 24 * block_count, 0, 8 * block_count * pieces - 1).astype(jnp.int32)
    oct_block = (first_block + oct_code // (8 * pieces)).astype(jnp.int32)
    octant = oct_code // pieces % 8
    piece_idx = oct_code % pieces
    start_two = (oct_block, zero_idx, (octant // 4 * half_len + 2 * piece_idx).astype(jnp.int32), (octant // 2 % 2 * half_len).astype(jnp.int32), (octant % 2 * half_len).astype(jnp.int32))
    slab = lax.dynamic_slice(volume, start_two, (1, 5, 2, half_len, half_len)).reshape(5, 2 * half_len * half_len)
    chosen = jnp.where(req_code < 24 * block_count, face_part, slab)
    return jnp.where(req_code < 0, 0.0, chosen)

def prolong(octants):
    grown = jnp.repeat(jnp.repeat(jnp.repeat(octants, 2, axis=2), 2, axis=3), 2, axis=4)
    return grown.reshape(octants.shape[0], 5, -1)

def coarse_ghost(payloads, weight, half_len):
    split = half_len * half_len
    earlier = payloads[..., :split]
    later = payloads[..., split:]
    mixed = (earlier + weight * (later - earlier)).reshape(payloads.shape[0], 5, half_len, half_len)
    return jnp.repeat(jnp.repeat(mixed, 2, axis=2), 2, axis=3)

def reflux_term(req_code, first_block, block_count, flux_volume, fine_avg):
    half_len = flux_volume.shape[3] // 2
    zero_idx = jnp.zeros((), jnp.int32)
    usable = (req_code >= 0) & (req_code < 24 * block_count)
    face_code = jnp.clip(req_code, 0, 24 * block_count - 1).astype(jnp.int32)
    block_idx = (first_block + face_code // 24).astype(jnp.int32)
    direction = face_code // 4 % 6
    quadrant = face_code % 4
    start = (block_idx, direction, zero_idx, (quadrant // 2 * half_len).astype(jnp.int32), (quadrant % 2 * half_len).astype(jnp.int32))
    coarse_part = lax.dynamic_slice(flux_volume, start, (1, 1, 5, half_len, half_len)).reshape(5, half_len * half_len)
    orient = jnp.where(direction % 2 == 1, 1.0, -1.0)
    return jnp.where(usable, orient * courant * (coarse_part - fine_avg), 0.0)

def spread_quadrants(register, block_count, half_len):
    shaped = register.reshape(block_count, 6, 2, 2, 5, half_len, half_len)
    return shaped.transpose(0, 1, 4, 2, 5, 3, 6).reshape(block_count, 6, 5, 2 * half_len, 2 * half_len)

def apply_layers(volume, layers):
    result = volume.at[:, :, 0].add(layers[:, 0]).at[:, :, -1].add(layers[:, 1])
    result = result.at[:, :, :, 0].add(layers[:, 2]).at[:, :, :, -1].add(layers[:, 3])
    result = result.at[:, :, :, :, 0].add(layers[:, 4]).at[:, :, :, :, -1].add(layers[:, 5])
    return result

def pick_rows(table, indices):
    return table[indices]

def reference(fine_old, send_left, send_right, new_source, face_source, request_slot, request_code, coarse_old, coarse_new, coarse_flux):
    edge_len = BS
    half_len = HALF
    coarse_vol = coarse_old.reshape(NCBLK, 5, edge_len, edge_len, edge_len)
    later_vol = coarse_new.reshape(NCBLK, 5, edge_len, edge_len, edge_len)
    old_faces = boundary_layers(coarse_vol)
    new_faces = boundary_layers(later_vol)
    device_of = jnp.arange(RANKS * REQ, dtype=jnp.int32) // REQ
    owner = device_of // PEERS * PEERS + request_slot // CAP

    def serve_one(req_code, owner_idx):
        return make_payload(req_code, owner_idx * CSLOTS, CSLOTS, coarse_vol, old_faces, new_faces, OCTP)
    answered = jax.vmap(serve_one)(request_code, owner).reshape(RANKS, REQ, 5, PATCH)
    octants = answered[:, FACEREQ:].reshape(RANKS * NEWB, OCTP, 5, 2, half_len, half_len)
    octants = octants.transpose(0, 2, 1, 3, 4, 5).reshape(RANKS * NEWB, 5, half_len, half_len, half_len)
    created = prolong(octants).reshape(RANKS, NEWB, 5, CELLS)
    old_blocks = fine_old.reshape(RANKS, SLOTS, 5, CELLS)
    lefts = jax.vmap(pick_rows)(old_blocks, send_left.reshape(RANKS, MOVE))
    rights = jax.vmap(pick_rows)(old_blocks, send_right.reshape(RANKS, MOVE))
    blank = jnp.zeros((1, MOVE, 5, CELLS), jnp.float32)
    from_left = jnp.concatenate([blank, rights[:-1]], axis=0)
    from_right = jnp.concatenate([lefts[1:], blank], axis=0)
    block_pool = jnp.concatenate([old_blocks, from_left, from_right, created], axis=1)
    regridded = jax.vmap(pick_rows)(block_pool, new_source.reshape(RANKS, SLOTS))
    fine_vol = regridded.reshape(RANKS, SLOTS, 5, edge_len, edge_len, edge_len)
    coarse_part = answered[:, :FACEREQ].reshape(RANKS * FACEREQ, 5, PATCH)
    sources = face_source.reshape(RANKS, SLOTS * 6)
    register = None
    for step_idx in range(2):
        layers = jax.vmap(boundary_layers)(fine_vol)
        empty = jnp.zeros_like(layers[:1])
        widened = jnp.concatenate([jnp.concatenate([empty, layers[:-1]], axis=0), layers, jnp.concatenate([layers[1:], empty], axis=0)], axis=1)
        ghost_coarse = coarse_ghost(coarse_part, 0.5 * step_idx, half_len).reshape(RANKS, FACEREQ, 5, edge_len, edge_len)
        ghost_pool = jnp.concatenate([widened.reshape(RANKS, 18 * SLOTS, 5, edge_len, edge_len), ghost_coarse], axis=1)
        ghosts = jax.vmap(pick_rows)(ghost_pool, sources).reshape(RANKS, SLOTS, 6, 5, edge_len, edge_len)
        fine_vol, borders = lax.map(lambda pair: advance(pair[0], pair[1]), (fine_vol, ghosts))
        register = borders if step_idx == 0 else register + borders
    averaged = register.reshape(RANKS, SLOTS * 6, 5, half_len, 2, half_len, 2).sum(axis=(4, 6)) / 8.0
    averaged = averaged.reshape(RANKS, SLOTS * 6, 5, half_len * half_len)
    targets = 18 * SLOTS + jnp.arange(FACEREQ, dtype=jnp.int32)
    matches = sources[:, None, :] == targets[None, :, None]
    face_index = lax.optimization_barrier(jnp.sum(jnp.where(matches, jnp.arange(SLOTS * 6, dtype=jnp.int32)[None, None, :], 0), axis=2)).astype(jnp.int32)
    outbound = jax.vmap(pick_rows)(averaged, face_index).reshape(RANKS * FACEREQ, 5, half_len * half_len)
    face_codes = request_code.reshape(RANKS, REQ)[:, :FACEREQ].reshape(-1)
    face_owner = owner.reshape(RANKS, REQ)[:, :FACEREQ].reshape(-1)
    flux_volume = coarse_flux.reshape(NCBLK, 6, 5, edge_len, edge_len)

    def correct_one(req_code, owner_idx, fine_avg):
        return reflux_term(req_code, owner_idx * CSLOTS, CSLOTS, flux_volume, fine_avg)
    corrections = jax.vmap(correct_one)(face_codes, face_owner, outbound)
    totals = jnp.zeros((NCBLK * 24, 5, half_len * half_len), jnp.float32).at[face_owner * (CSLOTS * 24) + face_codes].add(corrections)
    coarse_state = apply_layers(later_vol, spread_quadrants(totals, NCBLK, half_len)).reshape(NCBLK, 5, CELLS)
    fine_state = fine_vol.reshape(NBLK, 5, CELLS)
    return (fine_state, coarse_state)
```

```python
import functools

import jax
import jax.numpy as jnp
from jax import lax
from jax.experimental import pallas as pl
from jax.experimental.pallas import tpu as pltpu
from jax.sharding import PartitionSpec as P

MESH = pl.DeviceIdType.MESH
SLOTS = 6
CSLOTS = 4
CAP = 4
FACES = 36
FACEREQ = 6
REQ = 14
NEWB = 2
OCTP = 4
f32 = jnp.float32
i32 = jnp.int32


def pick(x, idx):
    return jnp.take_along_axis(x, idx, axis=1, mode="promise_in_bounds")


def loop(count, body):
    def step(i, carry):
        body(i)
        return carry

    lax.fori_loop(0, count, step, 0)


def lane_of(rows):
    return lax.broadcasted_iota(i32, (rows, 128), 1)


def merge_halves(first, second, rows):
    low = (lane_of(rows) & 15) < 8
    return (
        jnp.where(low, first, pltpu.roll(second, 8, 1)),
        jnp.where(low, pltpu.roll(first, 120, 1), second),
    )


def flux_and_speed(state, axis):
    density, energy = state[0], state[4]
    inverse = 1.0 / density
    kinetic = (state[1] * state[1] + state[2] * state[2] + state[3] * state[3]) * inverse
    pressure = 0.4 * energy - 0.2 * kinetic
    velocity = state[1 + axis] * inverse
    flux = [part * velocity for part in state]
    flux[1 + axis] = flux[1 + axis] + pressure
    flux[4] = flux[4] + pressure * velocity
    return flux, jnp.abs(velocity) + jnp.sqrt(1.4 * pressure * inverse)


def shifted_x(own, ghost_low, ghost_high):
    sub = lax.broadcasted_iota(i32, (4, 8, 128), 1)
    down = pltpu.roll(own, 2, 1)
    entering = pltpu.roll(ghost_low[3], 2, 0)
    low = jnp.where(sub < 2, jnp.concatenate([entering[None], down[:3]], axis=0), down)
    up = pltpu.roll(own, 6, 1)
    entering = pltpu.roll(ghost_high[0], 6, 0)
    high = jnp.where(sub >= 6, jnp.concatenate([up[1:], entering[None]], axis=0), up)
    return low, high


def swap_rows(value, odd):
    return jnp.where(odd, pltpu.roll(value, 1, 1), pltpu.roll(value, 7, 1))


def shifted_y(own, ghost_low, ghost_high):
    odd = (lax.broadcasted_iota(i32, (4, 8, 128), 1) & 1) == 1
    lane = lax.broadcasted_iota(i32, (4, 8, 128), 2)
    low = swap_rows(jnp.where(odd, ghost_low, own), odd)
    low = pltpu.roll(jnp.where(lane >= 112, low, own), 16, 2)
    high = swap_rows(jnp.where(odd, own, ghost_high), odd)
    high = pltpu.roll(jnp.where(lane < 16, high, own), 112, 2)
    return low, high


def shifted_z(own, ghost_low, ghost_high):
    z = lax.broadcasted_iota(i32, (4, 8, 128), 2) & 15
    low = jnp.where(z == 0, pltpu.roll(ghost_low, 113, 2), pltpu.roll(own, 1, 2))
    high = jnp.where(z == 15, pltpu.roll(ghost_high, 15, 2), pltpu.roll(own, 127, 2))
    return low, high


def advance_block(source, put, block, ghost_index):
    shape = (4, 8, 128)
    own = [source[block, c].reshape(shape) for c in range(5)]
    inverse = 1.0 / own[0]
    kinetic = (own[1] * own[1] + own[2] * own[2] + own[3] * own[3]) * inverse
    pressure = 0.4 * own[4] - 0.2 * kinetic
    sound = jnp.sqrt(1.4 * pressure * inverse)
    total = [None] * 5
    for axis, shifted in enumerate((shifted_x, shifted_y, shifted_z)):
        low_at = ghost_index[block * 6 + 2 * axis]
        high_at = ghost_index[block * 6 + 2 * axis + 1]
        low, high = [], []
        for c in range(5):
            below, above = shifted(
                own[c], source[low_at, c].reshape(shape), source[high_at, c].reshape(shape)
            )
            low.append(below)
            high.append(above)
        speed = jnp.abs(own[1 + axis] * inverse) + sound
        low_flux, low_speed = flux_and_speed(low, axis)
        high_flux, high_speed = flux_and_speed(high, axis)
        low_speed = jnp.maximum(low_speed, speed)
        high_speed = jnp.maximum(high_speed, speed)
        for c in range(5):
            part = high_flux[c] - low_flux[c]
            part = part + low_speed * (own[c] - low[c]) - high_speed * (high[c] - own[c])
            total[c] = part if axis == 0 else total[c] + part
    for c in range(5):
        put(block, c, (own[c] - 0.04 * total[c]).reshape(32, 128))


def kernel(
    sizes,
    send_left,
    send_right,
    new_source,
    face_source,
    request_slot,
    request_code,
    fine_hbm,
    old_hbm,
    new_hbm,
    flux_hbm,
    fine_out,
    coarse_out,
    fine_in,
    old_in,
    new_in,
    flux_in,
    codes_out,
    codes_in,
    codes_at,
    wants_out,
    wants_in,
    wants_at,
    ghost_index,
    face_at,
    slot_from,
    face_want,
    own_rows,
    made_rows,
    table_rows,
    own_flat,
    pool,
    moved,
    bundle,
    table,
    payload_out,
    payload_in,
    state_a,
    state_b,
    state_c,
    pick_index,
    pick_mask,
    spread_index,
    grow_index,
    faces_out_a,
    faces_out_b,
    faces_in_a,
    faces_in_b,
    edge_own,
    edge_coarse,
    register,
    average,
    parcel_out,
    parcel_in,
    gathered,
    code_rows,
    load_sem,
    local_sem,
    code_send,
    code_recv,
    want_send,
    want_recv,
    block_send,
    block_recv,
    payload_send,
    payload_recv,
    face_send,
    face_recv,
    parcel_send,
    parcel_recv,
):
    n_gx, n_gy, n_gz = sizes
    peers = n_gy * n_gz
    ranks = n_gx * peers
    gx, gy, gz = lax.axis_index("gx"), lax.axis_index("gy"), lax.axis_index("gz")
    me = gy * n_gz + gz
    rank = gx * peers + me

    def peer_at(step):
        index = lax.rem(me + step, peers)
        return index, (gx, index // n_gz, lax.rem(index, n_gz))

    def on_curve(index):
        return (index // peers, lax.rem(index // n_gz, n_gy), lax.rem(index, n_gz))

    beside = (on_curve(lax.rem(rank + ranks - 1, ranks)), on_curve(lax.rem(rank + 1, ranks)))

    loads = [
        pltpu.make_async_copy(fine_hbm, fine_in, load_sem.at[0]),
        pltpu.make_async_copy(old_hbm, old_in, load_sem.at[1]),
        pltpu.make_async_copy(new_hbm, new_in, load_sem.at[2]),
        pltpu.make_async_copy(flux_hbm, flux_in, load_sem.at[3]),
    ]
    for load in loads:
        load.start()

    faces_out, faces_in = (faces_out_a, faces_out_b), (faces_in_a, faces_in_b)
    barrier = pltpu.get_barrier_semaphore()

    def greet(step):
        pl.semaphore_signal(barrier, inc=1, device_id=peer_at(step + 1)[1], device_id_type=MESH)

    loop(peers - 1, greet)
    for device in beside:
        pl.semaphore_signal(barrier, inc=1, device_id=device, device_id_type=MESH)

    lane1 = lane_of(1)

    def build_codes(peer):
        row = jnp.full((1, 128), -1, i32)
        for r in range(REQ):
            row = jnp.where(lane1 + peer * CAP == request_slot[r], request_code[r], row)
        codes_out[peer] = jnp.where(lane1 < CAP, row, -1)

    loop(peers, build_codes)

    def scan(i, carry):
        count, wants, places = carry
        e = face_source[i // 6, lax.rem(i, 6)]
        is_left = e < FACES
        is_right = (e >= 2 * FACES) & (e < 3 * FACES)
        index = jnp.where(
            is_left,
            SLOTS + jnp.minimum(count[0], 2),
            jnp.where(
                is_right,
                SLOTS + 3 + jnp.minimum(count[1], 2),
                jnp.where(e >= 3 * FACES, SLOTS + 6 + e - 3 * FACES, (e - FACES) // 6),
            ),
        )
        ghost_index[i] = index
        new_wants = tuple(
            jnp.where(is_left & (count[0] == j), e, wants[j]) for j in range(3)
        ) + tuple(
            jnp.where(is_right & (count[1] == j), e - 2 * FACES, wants[3 + j]) for j in range(3)
        )
        new_places = tuple(
            jnp.where(e == 3 * FACES + r, i, places[r]) for r in range(FACEREQ)
        )
        new_count = (
            count[0] + jnp.where(is_left, 1, 0),
            count[1] + jnp.where(is_right, 1, 0),
        )
        return new_count, new_wants, new_places

    zero = jnp.int32(0)
    _, wants, places = lax.fori_loop(
        0, FACES, scan, ((zero, zero), (zero,) * 6, (zero,) * FACEREQ)
    )
    for r in range(FACEREQ):
        face_at[r] = places[r]
    for side in range(2):
        row = jnp.zeros((1, 128), i32)
        for j in range(3):
            row = jnp.where(lane1 == j, wants[3 * side + j], row)
        wants_out[side] = row

    def invert(slot):
        found = jnp.int32(0)
        for r in range(FACEREQ):
            found = jnp.where(request_slot[r] == slot, r, found)
        slot_from[slot] = found

    def rows_of(block, c):
        return pl.ds(pl.multiple_of((block * 5 + c) * 32, 32), 32)

    loads[0].wait()

    def unfold(i):
        c, k = i // 32, lax.rem(i, 32)
        value = fine_in[c, :, pl.ds(pl.multiple_of(k * 128, 128), 128)]
        own_rows[pl.ds(i, SLOTS, stride=160), :] = value

    loop(160, unfold)

    def split_own(block):
        for c in range(5):
            value = own_rows[rows_of(block, c), :]
            own_flat[block, c] = value
            pool[block, c] = value

    loop(SLOTS, split_own)
    for side, listed in enumerate((send_left, send_right)):
        for j in range(2):
            bundle[side, j] = own_flat[listed[j]]

    pl.semaphore_wait(barrier, peers + 1)

    def code_copy(step):
        index, device = peer_at(step)
        return pltpu.make_async_remote_copy(
            src_ref=codes_out.at[index],
            dst_ref=codes_in.at[me],
            send_sem=code_send.at[step],
            recv_sem=code_recv.at[step],
            device_id=device,
            device_id_type=MESH,
        )

    def start_codes(step):
        code_copy(step + 1).start()

    loop(peers - 1, start_codes)

    def beside_copy(side, source, target, send, recv):
        return pltpu.make_async_remote_copy(
            src_ref=source,
            dst_ref=target,
            send_sem=send,
            recv_sem=recv,
            device_id=beside[side],
            device_id_type=MESH,
        )

    want_copies = [
        beside_copy(
            side, wants_out.at[side], wants_in.at[1 - side], want_send.at[side], want_recv.at[1 - side]
        )
        for side in range(2)
    ]
    for copy in want_copies:
        copy.start()
    block_copies = [
        beside_copy(
            side,
            bundle.at[side],
            moved.at[1 - side],
            block_send.at[side],
            block_recv.at[1 - side],
        )
        for side in range(2)
    ]
    for copy in block_copies:
        copy.start()

    loads[1].wait()
    loads[2].wait()
    lane8, lane4 = lane_of(8), lane_of(4)

    def both(c, k):
        at = pl.ds(pl.multiple_of(k * 128, 128), 128)
        return old_in[c, :, at], new_in[c, :, at]

    def put_face(c, face, quadrant, value):
        table_rows[pl.ds((face * 4 + quadrant) * 8 + c, CSLOTS, stride=24 * 8), :] = value

    def fill_table(c):
        for side in range(2):
            for half in range(2):
                first, second = both(c, 30 * side + half)
                for low, value in enumerate(merge_halves(first, second, 4)):
                    put_face(c, side, half * 2 + low, value)
        for side in range(2):

            def fill_y(half, side=side):
                rows = jnp.zeros((8, 128), f32)
                for x in range(8):
                    value = jnp.concatenate(both(c, half * 16 + 2 * x + side), axis=0)
                    shift = (16 * x - 112 * side) % 128
                    value = value if shift == 0 else pltpu.roll(value, shift, 1)
                    rows = jnp.where((lane8 >> 4) == x, value, rows)
                for low, value in enumerate(merge_halves(rows[:4], rows[4:], 4)):
                    put_face(c, 2 + side, half * 2 + low, value)

            loop(2, fill_y)

            def fill_z(quadrant, side=side):
                rows = jnp.zeros((8, 128), f32)
                index = (lane8 & 7) * 16 + 15 * side
                for x in range(8):
                    k = (quadrant // 2) * 16 + 2 * x + lax.rem(quadrant, 2)
                    value = pick(jnp.concatenate(both(c, k), axis=0), index)
                    rows = jnp.where((lane8 >> 4) == x, value, rows)
                put_face(c, 4 + side, quadrant, jnp.where((lane4 & 15) < 8, rows[:4], rows[4:]))

            loop(4, fill_z)

        def fill_octant(i):
            half, pair = i // 8, lax.rem(i, 8)
            at = pl.multiple_of((4 * pair + half) * 128, 128)
            first = old_in[c, :, pl.ds(at, 128)]
            second = old_in[c, :, pl.ds(pl.multiple_of(at + 256, 128), 128)]
            for low, value in enumerate(merge_halves(first, second, 4)):
                code = 96 + ((pair // 4) * 4 + half * 2 + low) * 4 + lax.rem(pair, 4)
                table_rows[pl.ds(code * 8 + c, CSLOTS, stride=32 * 8), :] = value

        loop(16, fill_octant)

    loop(5, fill_table)

    def split_table(code):
        table[code] = table_rows[pl.ds(pl.multiple_of(code * 8, 8), 8), :]

    loop(224, split_table)
    loop(peers * CAP, invert)

    sub = lax.broadcasted_iota(i32, (32, 128), 0)
    lane = lax.broadcasted_iota(i32, (32, 128), 1)
    x, yh = sub >> 1, sub & 1
    for face in range(6):
        axis, side = face // 2, face % 2
        if axis == 0:
            pick_index[face] = lane8
        elif axis == 1:
            pick_index[face] = 112 * side + (lane8 & 15)
        else:
            pick_index[face] = (lane8 & 7) * 16 + 15 * side
        for half in range(2):
            if axis == 0:
                mask = sub == 30 * side + half
            else:
                mask = ((x >> 3) == half) & ((lane >> 4) == (x & 7))
                if axis == 1:
                    mask = mask & (yh == side)
                else:
                    mask = mask & (((lane >> 3) & 1) == yh)
            pick_mask[face, half] = jnp.where(mask, 1.0, 0.0)
    spread_index[0] = lane
    spread_index[1] = (x & 7) * 16 + (lane & 15)
    spread_index[2] = (x & 7) * 16 + 8 * yh + (lane >> 4)
    grow_index[0] = (4 * yh + (lane >> 5)) * 16 + ((lane & 15) >> 1)
    grow_index[1] = (x >> 1) * 16 + ((lane & 15) >> 1)
    grow_index[2] = (x >> 1) * 16 + 4 * yh + (lane >> 5)


    def wait_codes(step):
        code_copy(step + 1).wait()

    loop(peers - 1, wait_codes)
    codes_in[me] = codes_out[me]
    to_scalars = pltpu.make_async_copy(codes_in, codes_at, local_sem.at[0])
    to_scalars.start()
    to_scalars.wait()

    def answer(peer, place):
        code = jnp.maximum(codes_at[peer, 0, place], 0)
        return table[code][:5]

    def payload_copy(step):
        index, device = peer_at(step)
        return pltpu.make_async_remote_copy(
            src_ref=payload_out.at[pl.ds(step * CAP, CAP)],
            dst_ref=payload_in.at[pl.ds(me * CAP, CAP)],
            send_sem=payload_send.at[step],
            recv_sem=payload_recv.at[step],
            device_id=device,
            device_id_type=MESH,
        )

    def start_payload(step):
        index, _ = peer_at(step + 1)
        for place in range(CAP):
            payload_out[(step + 1) * CAP + place] = answer(index, place)
        payload_copy(step + 1).start()

    loop(peers - 1, start_payload)

    for copy in want_copies:
        copy.wait()
    to_scalars = pltpu.make_async_copy(wants_in, wants_at, local_sem.at[1])
    to_scalars.start()
    to_scalars.wait()
    for peer in range(peers):
        code_rows[pl.ds(peer, 1), :] = codes_in[peer]
    for copy in block_copies:
        copy.wait()
    for side in range(2):
        for j in range(2):
            pool[SLOTS + 2 * side + j] = moved[side, j]

    def wait_payload(step):
        payload_copy(step + 1).wait()

    loop(peers - 1, wait_payload)
    for place in range(CAP):
        payload_in[me * CAP + place] = answer(me, place)

    lane5 = lane_of(5)
    grow5 = [(4 * half + (lane5 >> 5)) * 16 + ((lane5 & 15) >> 1) for half in range(2)]
    for block in range(NEWB):
        for piece in range(OCTP):
            value = payload_in[request_slot[FACEREQ + block * OCTP + piece]]
            for part in range(2):
                for half in range(2):
                    grown = pick(value, grow5[half] + 8 * part)
                    for twin in range(2):
                        k = 2 * (4 * piece + 2 * part + twin) + half
                        made_rows[pl.ds(block * 160 + k, 5, stride=32), :] = grown

    for block in range(NEWB):
        for c in range(5):
            pool[10 + block, c] = made_rows[rows_of(block, c), :]

    def regrid(block):
        state_a[block] = pool[new_source[block]]

    loop(SLOTS, regrid)

    def take_face(state, face_id, put):
        block, face = face_id // 6, lax.rem(face_id, 6)
        index = pick_index[face]
        masks = [pick_mask[face, half].reshape(4, 8, 128) for half in range(2)]
        for c in range(5):
            value = state[block, c].reshape(4, 8, 128)
            picked = [pick(value[v], index) for v in range(4)]
            for half in range(2):
                rows = picked[0] * masks[half][0]
                for v in range(1, 4):
                    rows = rows + picked[v] * masks[half][v]
                put(c, half, jnp.sum(rows, axis=0, keepdims=True))

    def send_faces(step, state):
        def one(i):
            side, j = i // 3, lax.rem(i, 3)

            def put(c, half, row):
                faces_out[step][side, j, pl.ds(2 * c + half, 1), :] = row

            take_face(state, wants_at[side, 0, j], put)

        loop(6, one)
        copies = [
            beside_copy(
                side,
                faces_out[step].at[side],
                faces_in[step].at[1 - side],
                face_send.at[step, side],
                face_recv.at[step, 1 - side],
            )
            for side in range(2)
        ]
        for copy in copies:
            copy.start()
        return copies

    def take_edges(state):
        def one(r):
            def put(c, half, row):
                edge_own[c, pl.ds(2 * r + half, 1), :] = row

            take_face(state, face_at[r], put)

        loop(FACEREQ, one)

    def place_faces(step, state):
        def one(i):
            side, j = i // 3, lax.rem(i, 3)
            face = lax.rem(wants_out_face(side, j), 6)
            axis = face // 2
            index = spread_index[axis].reshape(4, 8, 128)
            odd = (lax.broadcasted_iota(i32, (8, 128), 0) & 1) == 1
            for c in range(5):
                first = jnp.broadcast_to(faces_in[step][side, j, pl.ds(2 * c, 1), :], (8, 128))
                second = jnp.broadcast_to(faces_in[step][side, j, pl.ds(2 * c + 1, 1), :], (8, 128))
                both_rows = jnp.where(odd, second, first)
                parts = []
                for v in range(4):
                    rows = jnp.where(axis == 0, both_rows, first if v < 2 else second)
                    parts.append(pick(rows, index[v]))
                state[SLOTS + i, c] = jnp.concatenate(parts, axis=0)

        loop(6, one)

    def wants_out_face(side, j):
        return face_want[side * 3 + j]

    for j in range(6):
        face_want[j] = wants[j]

    def register_step(step):
        axis_row = jnp.zeros((16, 128), i32)
        sign_row = jnp.zeros((16, 128), f32)
        row = lax.broadcasted_iota(i32, (16, 128), 0) >> 1
        for r in range(FACEREQ):
            face = lax.rem(face_at[r], 6)
            axis_row = jnp.where(row == r, face // 2, axis_row)
            sign_row = jnp.where(row == r, (2 * lax.rem(face, 2) - 1).astype(f32), sign_row)
        is_axis = [axis_row == axis for axis in range(3)]
        own = [edge_own[c] for c in range(5)]
        old = [edge_coarse[0, c] for c in range(5)]
        ghost = old
        if step == 1:
            ghost = [old[c] + 0.5 * (edge_coarse[1, c] - old[c]) for c in range(5)]

        def parts(state):
            inverse = 1.0 / state[0]
            normal = jnp.where(is_axis[0], state[1], jnp.where(is_axis[1], state[2], state[3]))
            kinetic = (state[1] * state[1] + state[2] * state[2] + state[3] * state[3]) * inverse
            pressure = 0.4 * state[4] - 0.2 * kinetic
            velocity = normal * inverse
            flux = [part * velocity for part in state]
            for axis in range(3):
                flux[1 + axis] = flux[1 + axis] + jnp.where(is_axis[axis], pressure, 0.0)
            flux[4] = flux[4] + pressure * velocity
            return flux, jnp.abs(velocity) + jnp.sqrt(1.4 * pressure * inverse)

        own_flux, own_speed = parts(own)
        ghost_flux, ghost_speed = parts(ghost)
        speed = jnp.maximum(own_speed, ghost_speed) * sign_row
        for c in range(5):
            value = 0.5 * (own_flux[c] + ghost_flux[c]) - 0.5 * speed * (ghost[c] - own[c])
            at = pl.ds(16 * c, 16)
            register[at, :] = value if step == 0 else register[at, :] + value

    copies = send_faces(0, state_a)
    edge_own[...] = jnp.ones((5, 16, 128), f32)
    edge_coarse[...] = jnp.ones((2, 5, 16, 128), f32)
    take_edges(state_a)

    def coarse_ghosts(r):
        slot = request_slot[r]
        axis = lax.rem(face_at[r], 6) // 2
        index = grow_index[axis].reshape(4, 8, 128)
        value = payload_in[slot]
        for when in range(2):
            for half in range(2):
                grown = pick(value, grow5[half] + 8 * when)
                for c in range(5):
                    edge_coarse[when, c, pl.ds(2 * r + half, 1), :] = grown[c : c + 1]
        for c in range(5):
            rows = jnp.broadcast_to(value[c : c + 1], (8, 128))
            old = jnp.concatenate([pick(rows, index[v]) for v in range(4)], axis=0)
            new = jnp.concatenate([pick(rows, index[v] + 8) for v in range(4)], axis=0)
            state_a[SLOTS + 6 + r, c] = old
            state_b[SLOTS + 6 + r, c] = old + 0.5 * (new - old)

    loop(FACEREQ, coarse_ghosts)
    register_step(0)
    for copy in copies:
        copy.wait()
    place_faces(0, state_a)

    def first_step(block):
        def put(block, c, value):
            state_b[block, c] = value

        advance_block(state_a, put, block, ghost_index)

    loop(SLOTS, first_step)

    copies = send_faces(1, state_b)
    take_edges(state_b)
    register_step(1)

    lane16 = lane_of(16)
    shrink = ((lane16 >> 4) & 3) * 32 + 2 * (lane16 & 7)
    for c in range(5):
        value = register[16 * c : 16 * c + 16, :]
        value = value + pltpu.roll(value, 127, 1)
        value = value + pltpu.roll(value, 112, 1)
        value = value * 0.125
        register[16 * c : 16 * c + 16, :] = jnp.concatenate(
            [pick(value[:8], shrink[:8]), pick(value[8:], shrink[8:])], axis=0
        )
    for r in range(FACEREQ):
        first = register[pl.ds(2 * r, 5, stride=16), :]
        second = register[pl.ds(2 * r + 1, 5, stride=16), :]
        average[r] = jnp.where(lane5 < 64, first, second)

    def parcel_copy(step):
        index, device = peer_at(step)
        return pltpu.make_async_remote_copy(
            src_ref=parcel_out.at[pl.ds(step * 2, 2)],
            dst_ref=parcel_in.at[pl.ds(me * 2, 2)],
            send_sem=parcel_send.at[step],
            recv_sem=parcel_recv.at[step],
            device_id=device,
            device_id_type=MESH,
        )

    def parcel(row):
        first = average[slot_from[2 * row]]
        second = average[slot_from[2 * row + 1]]
        return jnp.where((lane5 & 15) < 8, first, second)

    def start_parcel(step):
        index, _ = peer_at(step + 1)
        for pair in range(2):
            parcel_out[(step + 1) * 2 + pair] = parcel(index * 2 + pair)
        parcel_copy(step + 1).start()

    loop(peers - 1, start_parcel)

    for copy in copies:
        copy.wait()
    place_faces(1, state_b)

    def second_step(block):
        def put(block, c, value):
            state_c[rows_of(block, c), :] = value

        advance_block(state_b, put, block, ghost_index)

    loop(SLOTS, second_step)

    def fold(i):
        c, k = i // 32, lax.rem(i, 32)
        value = state_c[pl.ds(i, SLOTS, stride=160), :]
        fine_out[c, :, pl.ds(pl.multiple_of(k * 128, 128), 128)] = value

    loop(160, fold)

    target = lax.broadcasted_iota(i32, (peers, 128), 1)
    wanted = jnp.where(target < 24 * CSLOTS, (target & 3) * 24 + (target >> 2), -7)
    chosen = []
    for half in range(2):
        picks = [
            (jnp.broadcast_to(code_rows[:, 2 * pair + half : 2 * pair + half + 1], (peers, 128)) == wanted)
            for pair in range(2)
        ]
        chosen.append(
            jnp.concatenate([jnp.where(p, 1.0, 0.0) for p in picks], axis=0).astype(jnp.bfloat16)
        )

    def contract(left, right):
        return lax.dot_general(
            left, right, (((0,), (0,)), ((), ())), preferred_element_type=f32
        )

    ones = jnp.ones((2 * peers, 128), jnp.bfloat16)
    counts = contract(chosen[0], ones) + contract(chosen[1], ones)
    loads[3].wait()

    def wait_parcel(step):
        parcel_copy(step + 1).wait()

    loop(peers - 1, wait_parcel)
    for pair in range(2):
        parcel_in[me * 2 + pair] = parcel(me * 2 + pair)

    def line_up(peer):
        for pair in range(2):
            gathered[pl.ds(pair * peers + peer, 5, stride=2 * peers), :] = parcel_in[peer * 2 + pair]

    loop(peers, line_up)
    low8, low4 = (lane8 & 15) < 8, (lane4 & 15) < 8
    for c in range(5):
        value = gathered[pl.ds(c * 2 * peers, 2 * peers), :]
        coarse_part = value.astype(jnp.bfloat16)
        rest = (value - coarse_part.astype(f32)).astype(jnp.bfloat16)
        sums = [contract(chosen[h], coarse_part) + contract(chosen[h], rest) for h in range(2)]
        change = {}
        for face in range(6):
            scale = 0.08 if face % 2 else -0.08
            for half in range(2):
                at = (face * 2 + half) * 8
                first, second = sums[0][at : at + 8], sums[1][at : at + 8]
                count = counts[at : at + 8]
                lows = first + pltpu.roll(second, 120, 1)
                highs = second + pltpu.roll(first, 8, 1)
                total = jnp.where(low4, lows[:4], highs[4:])
                number = jnp.where(low4, count[:4], count[4:])
                flux = flux_in[face, c, :, pl.ds(half * 128, 128)]
                change[face, half] = scale * (number * flux - total)
        stacked = {
            face: jnp.concatenate([change[face, 0], change[face, 1]], axis=0) for face in range(2, 6)
        }
        for x8 in range(8):
            for yh8 in range(2):
                shift = (112 * yh8 - 16 * x8) % 128
                moved = stacked[2 + yh8]
                moved = moved if shift == 0 else pltpu.roll(moved, shift, 1)
                added = jnp.where((lane8 >> 4) == 7 * yh8, moved, 0.0)
                index = x8 * 16 + 8 * yh8 + (lane8 >> 4)
                added = added + jnp.where((lane8 & 15) == 0, pick(stacked[4], index), 0.0)
                added = added + jnp.where((lane8 & 15) == 15, pick(stacked[5], index), 0.0)
                for upper in range(2):
                    x_at = 8 * upper + x8
                    at = pl.ds((2 * x_at + yh8) * 128, 128)
                    value = new_in[c, :, at] + added[4 * upper : 4 * upper + 4]
                    if x_at == 0:
                        value = value + change[0, yh8]
                    if x_at == 15:
                        value = value + change[1, yh8]
                    coarse_out[c, :, at] = value


def on_device(sizes, fine_old, send_left, send_right, new_source, face_source, request_slot, request_code,
              coarse_old, coarse_new, coarse_flux):
    peers = sizes[1] * sizes[2]
    smem = pl.BlockSpec(memory_space=pltpu.SMEM)
    vmem = pl.BlockSpec(memory_space=pltpu.VMEM)
    hbm = pl.BlockSpec(memory_space=pl.ANY)
    dma = pltpu.SemaphoreType.DMA
    V = pltpu.VMEM
    fine, coarse = pl.pallas_call(
        functools.partial(kernel, sizes),
        out_shape=(
            jax.ShapeDtypeStruct((5, SLOTS, 4096), f32),
            jax.ShapeDtypeStruct((5, CSLOTS, 4096), f32),
        ),
        in_specs=[smem] * 6 + [hbm] * 4,
        out_specs=(vmem, vmem),
        scratch_shapes=[
            V((5, SLOTS, 4096), f32),
            V((5, CSLOTS, 4096), f32),
            V((5, CSLOTS, 4096), f32),
            V((6, 5, CSLOTS, 256), f32),
            V((peers, 1, 128), i32),
            V((peers, 1, 128), i32),
            pltpu.SMEM((peers, 1, 128), i32),
            V((2, 1, 128), i32),
            V((2, 1, 128), i32),
            pltpu.SMEM((2, 1, 128), i32),
            pltpu.SMEM((FACES,), i32),
            pltpu.SMEM((8,), i32),
            pltpu.SMEM((peers * CAP,), i32),
            pltpu.SMEM((8,), i32),
            V((8 * 160, 128), f32),
            V((416, 128), f32),
            V((2816, 128), f32),
            V((SLOTS, 5, 32, 128), f32),
            V((12, 5, 32, 128), f32),
            V((2, 2, 5, 32, 128), f32),
            V((2, 2, 5, 32, 128), f32),
            V((224, 8, 128), f32),
            V((peers * CAP, 5, 128), f32),
            V((peers * CAP, 5, 128), f32),
            V((18, 5, 32, 128), f32),
            V((18, 5, 32, 128), f32),
            V((8 * 160, 128), f32),
            V((6, 8, 128), i32),
            V((6, 2, 32, 128), f32),
            V((3, 32, 128), i32),
            V((3, 32, 128), i32),
            V((2, 3, 10, 128), f32),
            V((2, 3, 10, 128), f32),
            V((2, 3, 10, 128), f32),
            V((2, 3, 10, 128), f32),
            V((5, 16, 128), f32),
            V((2, 5, 16, 128), f32),
            V((128, 128), f32),
            V((FACEREQ, 5, 128), f32),
            V((peers * 2, 5, 128), f32),
            V((peers * 2, 5, 128), f32),
            V((8 * 2 * peers, 128), f32),
            V((peers, 128), i32),
            dma((4,)),
            dma((2,)),
            dma((peers,)),
            dma((peers,)),
            dma((2,)),
            dma((2,)),
            dma((2,)),
            dma((2,)),
            dma((peers,)),
            dma((peers,)),
            dma((2, 2)),
            dma((2, 2)),
            dma((peers,)),
            dma((peers,)),
        ],
        compiler_params=pltpu.CompilerParams(
            collective_id=0, has_side_effects=True, vmem_limit_bytes=40 * 1024 * 1024
        ),
    )(
        send_left,
        send_right,
        new_source,
        face_source,
        request_slot,
        request_code,
        jnp.transpose(fine_old, (1, 0, 2)),
        jnp.transpose(coarse_old, (1, 0, 2)),
        jnp.transpose(coarse_new, (1, 0, 2)),
        jnp.transpose(coarse_flux, (1, 2, 0, 3)),
    )
    return jnp.transpose(fine, (1, 0, 2)), jnp.transpose(coarse, (1, 0, 2))


def solution(mesh):
    sizes = (mesh.shape["gx"], mesh.shape["gy"], mesh.shape["gz"])
    every = ("gx", "gy", "gz")
    in_specs = (
        P(every, None, None),
        P(every),
        P(every),
        P(every),
        P(every, None),
        P(every),
        P(every),
        P(every, None, None),
        P(every, None, None),
        P(every, None, None, None),
    )
    out_specs = (P(every, None, None), P(every, None, None))
    return jax.shard_map(
        functools.partial(on_device, sizes), mesh=mesh, in_specs=in_specs, out_specs=out_specs, check_vma=False
    )
```

```python
import functools

import jax
import jax.numpy as jnp
from jax import lax
from jax.experimental import pallas as pl
from jax.experimental.pallas import tpu as pltpu
from jax.sharding import PartitionSpec as P

MESH = pl.DeviceIdType.MESH
SLOTS = 6
CSLOTS = 4
CAP = 4
FACES = 36
FACEREQ = 6
REQ = 14
NEWB = 2
OCTP = 4
f32 = jnp.float32
i32 = jnp.int32


def pick(x, idx):
    return jnp.take_along_axis(x, idx, axis=1, mode="promise_in_bounds")


def loop(count, body, unroll=1):
    def step(i, carry):
        for part in range(unroll):
            body(i * unroll + part)
        return carry

    lax.fori_loop(0, count // unroll, step, 0)
    for i in range(count - count % unroll, count):
        body(i)


def lane_of(rows):
    return lax.broadcasted_iota(i32, (rows, 128), 1)


def merge_halves(first, second, rows):
    low = (lane_of(rows) & 15) < 8
    return (
        jnp.where(low, first, pltpu.roll(second, 8, 1)),
        jnp.where(low, pltpu.roll(first, 120, 1), second),
    )


def flux_and_speed(state, axis):
    density, energy = state[0], state[4]
    inverse = 1.0 / density
    kinetic = (state[1] * state[1] + state[2] * state[2] + state[3] * state[3]) * inverse
    pressure = 0.4 * energy - 0.2 * kinetic
    velocity = state[1 + axis] * inverse
    flux = [part * velocity for part in state]
    flux[1 + axis] = flux[1 + axis] + pressure
    flux[4] = flux[4] + pressure * velocity
    return flux, jnp.abs(velocity) + jnp.sqrt(1.4 * pressure * inverse)


def shifted_x(own, ghost_low, ghost_high):
    sub = lax.broadcasted_iota(i32, (4, 8, 128), 1)
    down = pltpu.roll(own, 2, 1)
    entering = pltpu.roll(ghost_low[3], 2, 0)
    low = jnp.where(sub < 2, jnp.concatenate([entering[None], down[:3]], axis=0), down)
    up = pltpu.roll(own, 6, 1)
    entering = pltpu.roll(ghost_high[0], 6, 0)
    high = jnp.where(sub >= 6, jnp.concatenate([up[1:], entering[None]], axis=0), up)
    return low, high


def swap_rows(value, odd):
    return jnp.where(odd, pltpu.roll(value, 1, 1), pltpu.roll(value, 7, 1))


def shifted_y(own, ghost_low, ghost_high):
    odd = (lax.broadcasted_iota(i32, (4, 8, 128), 1) & 1) == 1
    lane = lax.broadcasted_iota(i32, (4, 8, 128), 2)
    low = swap_rows(jnp.where(odd, ghost_low, own), odd)
    low = pltpu.roll(jnp.where(lane >= 112, low, own), 16, 2)
    high = swap_rows(jnp.where(odd, own, ghost_high), odd)
    high = pltpu.roll(jnp.where(lane < 16, high, own), 112, 2)
    return low, high


def shifted_z(own, ghost_low, ghost_high):
    z = lax.broadcasted_iota(i32, (4, 8, 128), 2) & 15
    low = jnp.where(z == 0, pltpu.roll(ghost_low, 113, 2), pltpu.roll(own, 1, 2))
    high = jnp.where(z == 15, pltpu.roll(ghost_high, 15, 2), pltpu.roll(own, 127, 2))
    return low, high


def advance_block(source, put, block, ghost_index):
    shape = (4, 8, 128)
    own = [source[block, c].reshape(shape) for c in range(5)]
    inverse = 1.0 / own[0]
    kinetic = (own[1] * own[1] + own[2] * own[2] + own[3] * own[3]) * inverse
    pressure = 0.4 * own[4] - 0.2 * kinetic
    sound = jnp.sqrt(1.4 * pressure * inverse)
    total = [None] * 5
    for axis, shifted in enumerate((shifted_x, shifted_y, shifted_z)):
        low_at = ghost_index[block * 6 + 2 * axis]
        high_at = ghost_index[block * 6 + 2 * axis + 1]
        low, high = [], []
        for c in range(5):
            below, above = shifted(
                own[c], source[low_at, c].reshape(shape), source[high_at, c].reshape(shape)
            )
            low.append(below)
            high.append(above)
        speed = jnp.abs(own[1 + axis] * inverse) + sound
        low_flux, low_speed = flux_and_speed(low, axis)
        high_flux, high_speed = flux_and_speed(high, axis)
        low_speed = jnp.maximum(low_speed, speed)
        high_speed = jnp.maximum(high_speed, speed)
        for c in range(5):
            part = high_flux[c] - low_flux[c]
            part = part + low_speed * (own[c] - low[c]) - high_speed * (high[c] - own[c])
            total[c] = part if axis == 0 else total[c] + part
    for c in range(5):
        put(block, c, (own[c] - 0.04 * total[c]).reshape(32, 128))


def kernel(
    sizes,
    send_left,
    send_right,
    new_source,
    face_source,
    request_slot,
    request_code,
    fine_hbm,
    old_hbm,
    new_hbm,
    flux_hbm,
    fine_out,
    coarse_out,
    fine_in,
    old_in,
    new_in,
    flux_in,
    codes_out,
    codes_in,
    codes_at,
    wants_out,
    wants_in,
    wants_at,
    ghost_index,
    face_at,
    slot_from,
    face_want,
    own_rows,
    made_rows,
    table_rows,
    own_flat,
    pool,
    moved,
    bundle,
    table,
    payload_out,
    payload_in,
    state_a,
    state_b,
    state_c,
    pick_index,
    pick_mask,
    spread_index,
    grow_index,
    faces_out_a,
    faces_out_b,
    faces_in_a,
    faces_in_b,
    edge_own,
    edge_coarse,
    register,
    average,
    parcel_out,
    parcel_in,
    gathered,
    code_rows,
    load_sem,
    local_sem,
    code_send,
    code_recv,
    want_send,
    want_recv,
    block_send,
    block_recv,
    payload_send,
    payload_recv,
    face_send,
    face_recv,
    parcel_send,
    parcel_recv,
):
    n_gx, n_gy, n_gz = sizes
    peers = n_gy * n_gz
    ranks = n_gx * peers
    gx, gy, gz = lax.axis_index("gx"), lax.axis_index("gy"), lax.axis_index("gz")
    me = gy * n_gz + gz
    rank = gx * peers + me

    def peer_at(step):
        index = lax.rem(me + step, peers)
        return index, (gx, lax.div(index, n_gz), lax.rem(index, n_gz))

    def on_curve(index):
        return (lax.div(index, peers), lax.rem(lax.div(index, n_gz), n_gy), lax.rem(index, n_gz))

    beside = (on_curve(lax.rem(rank + ranks - 1, ranks)), on_curve(lax.rem(rank + 1, ranks)))

    faces_out, faces_in = (faces_out_a, faces_out_b), (faces_in_a, faces_in_b)
    barrier = pltpu.get_barrier_semaphore()

    def greet(step):
        pl.semaphore_signal(barrier, inc=1, device_id=peer_at(step + 1)[1], device_id_type=MESH)

    for step in range(peers - 1):
        greet(step)
    for device in beside:
        pl.semaphore_signal(barrier, inc=1, device_id=device, device_id_type=MESH)

    loads = [
        pltpu.make_async_copy(fine_hbm, fine_in, load_sem.at[0]),
        pltpu.make_async_copy(old_hbm, old_in, load_sem.at[1]),
        pltpu.make_async_copy(new_hbm, new_in, load_sem.at[2]),
        pltpu.make_async_copy(flux_hbm, flux_in, load_sem.at[3]),
    ]
    for load in loads:
        load.start()

    lane1 = lane_of(1)
    place_of = lax.broadcasted_iota(i32, (peers, 128), 0) * CAP + lane_of(peers)
    rows = jnp.full((peers, 128), -1, i32)
    for r in range(REQ):
        rows = jnp.where(place_of == request_slot[r], request_code[r], rows)
    code_rows[...] = jnp.where(lane_of(peers) < CAP, rows, -1)
    for peer in range(peers):
        codes_out[peer] = code_rows[pl.ds(peer, 1), :]

    pl.semaphore_wait(barrier, peers + 1)

    def code_copy(step):
        index, device = peer_at(step)
        return pltpu.make_async_remote_copy(
            src_ref=codes_out.at[index],
            dst_ref=codes_in.at[me],
            send_sem=code_send.at[step],
            recv_sem=code_recv.at[step],
            device_id=device,
            device_id_type=MESH,
        )

    def start_codes(step):
        code_copy(step + 1).start()

    for step in range(peers - 1):
        start_codes(step)

    def rows_of(block, c):
        return pl.ds(pl.multiple_of((block * 5 + c) * 32, 32), 32)

    loads[0].wait()

    def unfold(i):
        c, k = lax.div(i, 32), lax.rem(i, 32)
        value = fine_in[c, :, pl.ds(pl.multiple_of(k * 128, 128), 128)]
        own_rows[pl.ds(i, SLOTS, stride=160), :] = value

    loop(160, unfold, 16)

    def split_own(block):
        for c in range(5):
            value = own_rows[rows_of(block, c), :]
            own_flat[block, c] = value
            pool[block, c] = value

    loop(SLOTS, split_own, 2)
    for side, listed in enumerate((send_left, send_right)):
        for j in range(2):
            bundle[side, j] = own_flat[listed[j]]

    def beside_copy(side, source, target, send, recv):
        return pltpu.make_async_remote_copy(
            src_ref=source,
            dst_ref=target,
            send_sem=send,
            recv_sem=recv,
            device_id=beside[side],
            device_id_type=MESH,
        )

    block_copies = [
        beside_copy(
            side,
            bundle.at[side],
            moved.at[1 - side],
            block_send.at[side],
            block_recv.at[1 - side],
        )
        for side in range(2)
    ]
    for copy in block_copies:
        copy.start()

    loads[1].wait()
    loads[2].wait()
    lane8, lane4 = lane_of(8), lane_of(4)

    def both(c, k):
        at = pl.ds(k * 128, 128)
        return old_in[c, :, at], new_in[c, :, at]

    def put_face(c, face, quadrant, value):
        table_rows[pl.ds((face * 4 + quadrant) * 8 + c, CSLOTS, stride=24 * 8), :] = value

    def fill_table(c):
        for side in range(2):
            for half in range(2):
                first, second = both(c, 30 * side + half)
                for low, value in enumerate(merge_halves(first, second, 4)):
                    put_face(c, side, half * 2 + low, value)
        for side in range(2):

            def fill_y(half, side=side):
                rows = jnp.zeros((8, 128), f32)
                for x in range(8):
                    value = jnp.concatenate(both(c, half * 16 + 2 * x + side), axis=0)
                    shift = (16 * x - 112 * side) % 128
                    value = value if shift == 0 else pltpu.roll(value, shift, 1)
                    rows = jnp.where((lane8 >> 4) == x, value, rows)
                for low, value in enumerate(merge_halves(rows[:4], rows[4:], 4)):
                    put_face(c, 2 + side, half * 2 + low, value)

            for half in range(2):
                fill_y(half)

            def fill_z(quadrant, side=side):
                rows = jnp.zeros((8, 128), f32)
                index = (lane8 & 7) * 16 + 15 * side
                for x in range(8):
                    k = (quadrant // 2) * 16 + 2 * x + quadrant % 2
                    value = pick(jnp.concatenate(both(c, k), axis=0), index)
                    rows = jnp.where((lane8 >> 4) == x, value, rows)
                put_face(c, 4 + side, quadrant, jnp.where((lane4 & 15) < 8, rows[:4], rows[4:]))

            for quadrant in range(4):
                fill_z(quadrant)

        def fill_octant(i):
            half, pair = i // 8, i % 8
            at = (4 * pair + half) * 128
            first = old_in[c, :, pl.ds(at, 128)]
            second = old_in[c, :, pl.ds(at + 256, 128)]
            for low, value in enumerate(merge_halves(first, second, 4)):
                code = 96 + ((pair // 4) * 4 + half * 2 + low) * 4 + pair % 4
                table_rows[pl.ds(code * 8 + c, CSLOTS, stride=32 * 8), :] = value

        for i in range(16):
            fill_octant(i)

    loop(5, fill_table)

    def split_table(code):
        table[code] = table_rows[pl.ds(pl.multiple_of(code * 8, 8), 8), :]

    loop(224, split_table, 16)

    def wait_codes(step):
        code_copy(step + 1).wait()

    loop(peers - 1, wait_codes)
    codes_in[me] = codes_out[me]
    to_scalars = pltpu.make_async_copy(codes_in, codes_at, local_sem.at[0])
    to_scalars.start()
    to_scalars.wait()

    def answer(peer, place):
        code = jnp.maximum(codes_at[peer, 0, place], 0)
        return table[code][:5]

    def payload_copy(step):
        index, device = peer_at(step)
        return pltpu.make_async_remote_copy(
            src_ref=payload_out.at[pl.ds(step * CAP, CAP)],
            dst_ref=payload_in.at[pl.ds(me * CAP, CAP)],
            send_sem=payload_send.at[step],
            recv_sem=payload_recv.at[step],
            device_id=device,
            device_id_type=MESH,
        )

    def start_payload(step):
        index, _ = peer_at(step + 1)
        for place in range(CAP):
            payload_out[(step + 1) * CAP + place] = answer(index, place)
        payload_copy(step + 1).start()

    loop(peers - 1, start_payload, 4)

    def scan(i, carry):
        count, wants, places = carry
        e = face_source[lax.div(i, 6), lax.rem(i, 6)]
        is_left = e < FACES
        is_right = (e >= 2 * FACES) & (e < 3 * FACES)
        index = jnp.where(
            is_left,
            SLOTS + jnp.minimum(count[0], 2),
            jnp.where(
                is_right,
                SLOTS + 3 + jnp.minimum(count[1], 2),
                jnp.where(e >= 3 * FACES, SLOTS + 6 + e - 3 * FACES, lax.div(jnp.maximum(e - FACES, 0), 6)),
            ),
        )
        ghost_index[i] = index
        new_wants = tuple(
            jnp.where(is_left & (count[0] == j), e, wants[j]) for j in range(3)
        ) + tuple(
            jnp.where(is_right & (count[1] == j), e - 2 * FACES, wants[3 + j]) for j in range(3)
        )
        new_places = tuple(
            jnp.where(e == 3 * FACES + r, i, places[r]) for r in range(FACEREQ)
        )
        new_count = (
            count[0] + jnp.where(is_left, 1, 0),
            count[1] + jnp.where(is_right, 1, 0),
        )
        return new_count, new_wants, new_places

    zero = jnp.int32(0)
    _, wants, places = lax.fori_loop(
        0, FACES, scan, ((zero, zero), (zero,) * 6, (zero,) * FACEREQ)
    )
    for r in range(FACEREQ):
        face_at[r] = places[r]
    for side in range(2):
        row = jnp.zeros((1, 128), i32)
        for j in range(3):
            row = jnp.where(lane1 == j, wants[3 * side + j], row)
        wants_out[side] = row

    def invert(slot):
        found = jnp.int32(0)
        for r in range(FACEREQ):
            found = jnp.where(request_slot[r] == slot, r, found)
        slot_from[slot] = found

    want_copies = [
        beside_copy(
            side, wants_out.at[side], wants_in.at[1 - side], want_send.at[side], want_recv.at[1 - side]
        )
        for side in range(2)
    ]
    for copy in want_copies:
        copy.start()
    sub = lax.broadcasted_iota(i32, (32, 128), 0)
    lane = lax.broadcasted_iota(i32, (32, 128), 1)
    x, yh = sub >> 1, sub & 1
    for face in range(6):
        axis, side = face // 2, face % 2
        if axis == 0:
            pick_index[face] = lane8
        elif axis == 1:
            pick_index[face] = 112 * side + (lane8 & 15)
        else:
            pick_index[face] = (lane8 & 7) * 16 + 15 * side
        for half in range(2):
            if axis == 0:
                mask = sub == 30 * side + half
            else:
                mask = ((x >> 3) == half) & ((lane >> 4) == (x & 7))
                if axis == 1:
                    mask = mask & (yh == side)
                else:
                    mask = mask & (((lane >> 3) & 1) == yh)
            pick_mask[face, half] = jnp.where(mask, 1.0, 0.0)
    spread_index[0] = lane
    spread_index[1] = (x & 7) * 16 + (lane & 15)
    spread_index[2] = (x & 7) * 16 + 8 * yh + (lane >> 4)
    grow_index[0] = (4 * yh + (lane >> 5)) * 16 + ((lane & 15) >> 1)
    grow_index[1] = (x >> 1) * 16 + ((lane & 15) >> 1)
    grow_index[2] = (x >> 1) * 16 + 4 * yh + (lane >> 5)

    loop(peers * CAP, invert, 8)

    for copy in want_copies:
        copy.wait()
    to_scalars = pltpu.make_async_copy(wants_in, wants_at, local_sem.at[1])
    to_scalars.start()
    to_scalars.wait()
    for peer in range(peers):
        code_rows[pl.ds(peer, 1), :] = codes_in[peer]
    for copy in block_copies:
        copy.wait()
    for side in range(2):
        for j in range(2):
            pool[SLOTS + 2 * side + j] = moved[side, j]

    def wait_payload(step):
        payload_copy(step + 1).wait()

    loop(peers - 1, wait_payload)
    for place in range(CAP):
        payload_in[me * CAP + place] = answer(me, place)

    lane5 = lane_of(5)
    grow5 = [(4 * half + (lane5 >> 5)) * 16 + ((lane5 & 15) >> 1) for half in range(2)]
    for block in range(NEWB):
        for piece in range(OCTP):
            value = payload_in[request_slot[FACEREQ + block * OCTP + piece]]
            for part in range(2):
                for half in range(2):
                    grown = pick(value, grow5[half] + 8 * part)
                    for twin in range(2):
                        k = 2 * (4 * piece + 2 * part + twin) + half
                        made_rows[pl.ds(block * 160 + k, 5, stride=32), :] = grown

    for block in range(NEWB):
        for c in range(5):
            pool[10 + block, c] = made_rows[rows_of(block, c), :]

    def regrid(block):
        state_a[block] = pool[new_source[block]]

    loop(SLOTS, regrid, 2)

    def take_face(state, face_id, put):
        block, face = lax.div(face_id, 6), lax.rem(face_id, 6)
        index = pick_index[face]
        masks = [pick_mask[face, half].reshape(4, 8, 128) for half in range(2)]
        for c in range(5):
            value = state[block, c].reshape(4, 8, 128)
            picked = [pick(value[v], index) for v in range(4)]
            for half in range(2):
                rows = picked[0] * masks[half][0]
                for v in range(1, 4):
                    rows = rows + picked[v] * masks[half][v]
                put(c, half, jnp.sum(rows, axis=0, keepdims=True))

    def send_faces(step, state):
        def one(i):
            side, j = (i // 3, i % 3) if isinstance(i, int) else (lax.div(i, 3), lax.rem(i, 3))

            def put(c, half, row):
                faces_out[step][side, j, pl.ds(2 * c + half, 1), :] = row

            take_face(state, wants_at[side, 0, j], put)

        loop(6, one, 3)
        copies = [
            beside_copy(
                side,
                faces_out[step].at[side],
                faces_in[step].at[1 - side],
                face_send.at[step, side],
                face_recv.at[step, 1 - side],
            )
            for side in range(2)
        ]
        for copy in copies:
            copy.start()
        return copies

    def take_edges(state):
        def one(r):
            def put(c, half, row):
                edge_own[c, pl.ds(2 * r + half, 1), :] = row

            take_face(state, face_at[r], put)

        loop(FACEREQ, one, 3)

    def place_faces(step, state):
        def one(i):
            side, j = (i // 3, i % 3) if isinstance(i, int) else (lax.div(i, 3), lax.rem(i, 3))
            face = lax.rem(wants_out_face(side, j), 6)
            axis = lax.div(face, 2)
            index = spread_index[axis].reshape(4, 8, 128)
            odd = (lax.broadcasted_iota(i32, (8, 128), 0) & 1) == 1
            for c in range(5):
                first = jnp.broadcast_to(faces_in[step][side, j, pl.ds(2 * c, 1), :], (8, 128))
                second = jnp.broadcast_to(faces_in[step][side, j, pl.ds(2 * c + 1, 1), :], (8, 128))
                both_rows = jnp.where(odd, second, first)
                parts = []
                for v in range(4):
                    rows = jnp.where(axis == 0, both_rows, first if v < 2 else second)
                    parts.append(pick(rows, index[v]))
                state[SLOTS + i, c] = jnp.concatenate(parts, axis=0)

        loop(6, one, 3)

    def wants_out_face(side, j):
        return face_want[side * 3 + j]

    for j in range(6):
        face_want[j] = wants[j]

    def register_step(step):
        axis_row = jnp.zeros((16, 128), i32)
        sign_row = jnp.zeros((16, 128), f32)
        row = lax.broadcasted_iota(i32, (16, 128), 0) >> 1
        for r in range(FACEREQ):
            face = lax.rem(face_at[r], 6)
            axis_row = jnp.where(row == r, lax.div(face, 2), axis_row)
            sign_row = jnp.where(row == r, (2 * lax.rem(face, 2) - 1).astype(f32), sign_row)
        is_axis = [axis_row == axis for axis in range(3)]
        own = [edge_own[c] for c in range(5)]
        old = [edge_coarse[0, c] for c in range(5)]
        ghost = old
        if step == 1:
            ghost = [old[c] + 0.5 * (edge_coarse[1, c] - old[c]) for c in range(5)]

        def parts(state):
            inverse = 1.0 / state[0]
            normal = jnp.where(is_axis[0], state[1], jnp.where(is_axis[1], state[2], state[3]))
            kinetic = (state[1] * state[1] + state[2] * state[2] + state[3] * state[3]) * inverse
            pressure = 0.4 * state[4] - 0.2 * kinetic
            velocity = normal * inverse
            flux = [part * velocity for part in state]
            for axis in range(3):
                flux[1 + axis] = flux[1 + axis] + jnp.where(is_axis[axis], pressure, 0.0)
            flux[4] = flux[4] + pressure * velocity
            return flux, jnp.abs(velocity) + jnp.sqrt(1.4 * pressure * inverse)

        own_flux, own_speed = parts(own)
        ghost_flux, ghost_speed = parts(ghost)
        speed = jnp.maximum(own_speed, ghost_speed) * sign_row
        for c in range(5):
            value = 0.5 * (own_flux[c] + ghost_flux[c]) - 0.5 * speed * (ghost[c] - own[c])
            at = pl.ds(16 * c, 16)
            register[at, :] = value if step == 0 else register[at, :] + value

    copies = send_faces(0, state_a)
    edge_own[...] = jnp.ones((5, 16, 128), f32)
    edge_coarse[...] = jnp.ones((2, 5, 16, 128), f32)
    take_edges(state_a)

    def coarse_ghosts(r):
        slot = request_slot[r]
        axis = lax.div(lax.rem(face_at[r], 6), 2)
        index = grow_index[axis].reshape(4, 8, 128)
        value = payload_in[slot]
        for when in range(2):
            for half in range(2):
                grown = pick(value, grow5[half] + 8 * when)
                for c in range(5):
                    edge_coarse[when, c, pl.ds(2 * r + half, 1), :] = grown[c : c + 1]
        for c in range(5):
            rows = jnp.broadcast_to(value[c : c + 1], (8, 128))
            old = jnp.concatenate([pick(rows, index[v]) for v in range(4)], axis=0)
            new = jnp.concatenate([pick(rows, index[v] + 8) for v in range(4)], axis=0)
            state_a[SLOTS + 6 + r, c] = old
            state_b[SLOTS + 6 + r, c] = old + 0.5 * (new - old)

    loop(FACEREQ, coarse_ghosts, 2)
    register_step(0)
    for copy in copies:
        copy.wait()
    place_faces(0, state_a)

    def first_step(block):
        def put(block, c, value):
            state_b[block, c] = value

        advance_block(state_a, put, block, ghost_index)

    loop(SLOTS, first_step)

    copies = send_faces(1, state_b)
    take_edges(state_b)
    register_step(1)

    lane16 = lane_of(16)
    shrink = ((lane16 >> 4) & 3) * 32 + 2 * (lane16 & 7)
    for c in range(5):
        value = register[16 * c : 16 * c + 16, :]
        value = value + pltpu.roll(value, 127, 1)
        value = value + pltpu.roll(value, 112, 1)
        value = value * 0.125
        register[16 * c : 16 * c + 16, :] = jnp.concatenate(
            [pick(value[:8], shrink[:8]), pick(value[8:], shrink[8:])], axis=0
        )
    for r in range(FACEREQ):
        first = register[pl.ds(2 * r, 5, stride=16), :]
        second = register[pl.ds(2 * r + 1, 5, stride=16), :]
        average[r] = jnp.where(lane5 < 64, first, second)

    def parcel_copy(step):
        index, device = peer_at(step)
        return pltpu.make_async_remote_copy(
            src_ref=parcel_out.at[pl.ds(step * 2, 2)],
            dst_ref=parcel_in.at[pl.ds(me * 2, 2)],
            send_sem=parcel_send.at[step],
            recv_sem=parcel_recv.at[step],
            device_id=device,
            device_id_type=MESH,
        )

    def parcel(row):
        first = average[slot_from[2 * row]]
        second = average[slot_from[2 * row + 1]]
        return jnp.where((lane5 & 15) < 8, first, second)

    def start_parcel(step):
        index, _ = peer_at(step + 1)
        for pair in range(2):
            parcel_out[(step + 1) * 2 + pair] = parcel(index * 2 + pair)
        parcel_copy(step + 1).start()

    loop(peers - 1, start_parcel, 4)

    for copy in copies:
        copy.wait()
    place_faces(1, state_b)

    def second_step(block):
        def put(block, c, value):
            state_c[rows_of(block, c), :] = value

        advance_block(state_b, put, block, ghost_index)

    loop(SLOTS, second_step)

    def fold(i):
        c, k = lax.div(i, 32), lax.rem(i, 32)
        value = state_c[pl.ds(i, SLOTS, stride=160), :]
        fine_out[c, :, pl.ds(pl.multiple_of(k * 128, 128), 128)] = value

    loop(160, fold, 16)

    target = lax.broadcasted_iota(i32, (peers, 128), 1)
    wanted = jnp.where(target < 24 * CSLOTS, (target & 3) * 24 + (target >> 2), -7)
    chosen = []
    for half in range(2):
        picks = [
            (jnp.broadcast_to(code_rows[:, 2 * pair + half : 2 * pair + half + 1], (peers, 128)) == wanted)
            for pair in range(2)
        ]
        chosen.append(
            jnp.concatenate([jnp.where(p, 1.0, 0.0) for p in picks], axis=0).astype(jnp.bfloat16)
        )

    def contract(left, right):
        return lax.dot_general(
            left, right, (((0,), (0,)), ((), ())), preferred_element_type=f32
        )

    ones = jnp.ones((2 * peers, 128), jnp.bfloat16)
    counts = contract(chosen[0], ones) + contract(chosen[1], ones)
    loads[3].wait()

    def wait_parcel(step):
        parcel_copy(step + 1).wait()

    loop(peers - 1, wait_parcel)
    for pair in range(2):
        parcel_in[me * 2 + pair] = parcel(me * 2 + pair)

    def line_up(peer):
        for pair in range(2):
            gathered[pl.ds(pair * peers + peer, 5, stride=2 * peers), :] = parcel_in[peer * 2 + pair]

    loop(peers, line_up, 8)
    low8, low4 = (lane8 & 15) < 8, (lane4 & 15) < 8
    for c in range(5):
        value = gathered[pl.ds(c * 2 * peers, 2 * peers), :]
        coarse_part = value.astype(jnp.bfloat16)
        rest = (value - coarse_part.astype(f32)).astype(jnp.bfloat16)
        sums = [contract(chosen[h], coarse_part) + contract(chosen[h], rest) for h in range(2)]
        change = {}
        for face in range(6):
            scale = 0.08 if face % 2 else -0.08
            for half in range(2):
                at = (face * 2 + half) * 8
                first, second = sums[0][at : at + 8], sums[1][at : at + 8]
                count = counts[at : at + 8]
                lows = first + pltpu.roll(second, 120, 1)
                highs = second + pltpu.roll(first, 8, 1)
                total = jnp.where(low4, lows[:4], highs[4:])
                number = jnp.where(low4, count[:4], count[4:])
                flux = flux_in[face, c, :, pl.ds(half * 128, 128)]
                change[face, half] = scale * (number * flux - total)
        stacked = {
            face: jnp.concatenate([change[face, 0], change[face, 1]], axis=0) for face in range(2, 6)
        }
        for x8 in range(8):
            for yh8 in range(2):
                shift = (112 * yh8 - 16 * x8) % 128
                moved = stacked[2 + yh8]
                moved = moved if shift == 0 else pltpu.roll(moved, shift, 1)
                added = jnp.where((lane8 >> 4) == 7 * yh8, moved, 0.0)
                index = x8 * 16 + 8 * yh8 + (lane8 >> 4)
                added = added + jnp.where((lane8 & 15) == 0, pick(stacked[4], index), 0.0)
                added = added + jnp.where((lane8 & 15) == 15, pick(stacked[5], index), 0.0)
                for upper in range(2):
                    x_at = 8 * upper + x8
                    at = pl.ds((2 * x_at + yh8) * 128, 128)
                    value = new_in[c, :, at] + added[4 * upper : 4 * upper + 4]
                    if x_at == 0:
                        value = value + change[0, yh8]
                    if x_at == 15:
                        value = value + change[1, yh8]
                    coarse_out[c, :, at] = value


def on_device(sizes, fine_old, send_left, send_right, new_source, face_source, request_slot, request_code,
              coarse_old, coarse_new, coarse_flux):
    peers = sizes[1] * sizes[2]
    smem = pl.BlockSpec(memory_space=pltpu.SMEM)
    vmem = pl.BlockSpec(memory_space=pltpu.VMEM)
    hbm = pl.BlockSpec(memory_space=pltpu.HBM)
    dma = pltpu.SemaphoreType.DMA
    V = pltpu.VMEM
    fine, coarse = pl.pallas_call(
        functools.partial(kernel, sizes),
        out_shape=(
            jax.ShapeDtypeStruct((5, SLOTS, 4096), f32),
            jax.ShapeDtypeStruct((5, CSLOTS, 4096), f32),
        ),
        in_specs=[smem] * 6 + [hbm] * 4,
        out_specs=(vmem, vmem),
        scratch_shapes=[
            V((5, SLOTS, 4096), f32),
            V((5, CSLOTS, 4096), f32),
            V((5, CSLOTS, 4096), f32),
            V((6, 5, CSLOTS, 256), f32),
            V((peers, 1, 128), i32),
            V((peers, 1, 128), i32),
            pltpu.SMEM((peers, 1, 128), i32),
            V((2, 1, 128), i32),
            V((2, 1, 128), i32),
            pltpu.SMEM((2, 1, 128), i32),
            pltpu.SMEM((FACES,), i32),
            pltpu.SMEM((8,), i32),
            pltpu.SMEM((peers * CAP,), i32),
            pltpu.SMEM((8,), i32),
            V((8 * 160, 128), f32),
            V((416, 128), f32),
            V((2816, 128), f32),
            V((SLOTS, 5, 32, 128), f32),
            V((12, 5, 32, 128), f32),
            V((2, 2, 5, 32, 128), f32),
            V((2, 2, 5, 32, 128), f32),
            V((224, 8, 128), f32),
            V((peers * CAP, 5, 128), f32),
            V((peers * CAP, 5, 128), f32),
            V((18, 5, 32, 128), f32),
            V((18, 5, 32, 128), f32),
            V((8 * 160, 128), f32),
            V((6, 8, 128), i32),
            V((6, 2, 32, 128), f32),
            V((3, 32, 128), i32),
            V((3, 32, 128), i32),
            V((2, 3, 10, 128), f32),
            V((2, 3, 10, 128), f32),
            V((2, 3, 10, 128), f32),
            V((2, 3, 10, 128), f32),
            V((5, 16, 128), f32),
            V((2, 5, 16, 128), f32),
            V((128, 128), f32),
            V((FACEREQ, 5, 128), f32),
            V((peers * 2, 5, 128), f32),
            V((peers * 2, 5, 128), f32),
            V((8 * 2 * peers, 128), f32),
            V((peers, 128), i32),
            dma((4,)),
            dma((2,)),
            dma((peers,)),
            dma((peers,)),
            dma((2,)),
            dma((2,)),
            dma((2,)),
            dma((2,)),
            dma((peers,)),
            dma((peers,)),
            dma((2, 2)),
            dma((2, 2)),
            dma((peers,)),
            dma((peers,)),
        ],
        compiler_params=pltpu.CompilerParams(
            collective_id=0, has_side_effects=True, vmem_limit_bytes=40 * 1024 * 1024
        ),
    )(
        send_left,
        send_right,
        new_source,
        face_source,
        request_slot,
        request_code,
        jnp.transpose(fine_old, (1, 0, 2)),
        jnp.transpose(coarse_old, (1, 0, 2)),
        jnp.transpose(coarse_new, (1, 0, 2)),
        jnp.transpose(coarse_flux, (1, 2, 0, 3)),
    )
    return jnp.transpose(fine, (1, 0, 2)), jnp.transpose(coarse, (1, 0, 2))


def solution(mesh):
    sizes = (mesh.shape["gx"], mesh.shape["gy"], mesh.shape["gz"])
    every = ("gx", "gy", "gz")
    in_specs = (
        P(every, None, None),
        P(every),
        P(every),
        P(every),
        P(every, None),
        P(every),
        P(every),
        P(every, None, None),
        P(every, None, None),
        P(every, None, None, None),
    )
    out_specs = (P(every, None, None), P(every, None, None))
    return jax.shard_map(
        functools.partial(on_device, sizes), mesh=mesh, in_specs=in_specs, out_specs=out_specs, check_vma=False
    )
```

```python
import functools

import jax
import jax.numpy as jnp
from jax import lax
from jax.experimental import pallas as pl
from jax.experimental.pallas import tpu as pltpu
from jax.sharding import PartitionSpec as P

MESH = pl.DeviceIdType.MESH
SLOTS = 6
CSLOTS = 4
CAP = 4
FACES = 36
FACEREQ = 6
REQ = 14
NEWB = 2
OCTP = 4
f32 = jnp.float32
i32 = jnp.int32


def pick(x, idx):
    return jnp.take_along_axis(x, idx, axis=1, mode="promise_in_bounds")


def loop(count, body, unroll=1):
    def step(i, carry):
        for part in range(unroll):
            body(i * unroll + part)
        return carry

    lax.fori_loop(0, count // unroll, step, 0)
    for i in range(count - count % unroll, count):
        body(i)


def lane_of(rows):
    return lax.broadcasted_iota(i32, (rows, 128), 1)


def merge_halves(first, second, rows):
    low = (lane_of(rows) & 15) < 8
    return (
        jnp.where(low, first, pltpu.roll(second, 8, 1)),
        jnp.where(low, pltpu.roll(first, 120, 1), second),
    )


def flux_and_speed(state, axis):
    density, energy = state[0], state[4]
    inverse = 1.0 / density
    kinetic = (state[1] * state[1] + state[2] * state[2] + state[3] * state[3]) * inverse
    pressure = 0.4 * energy - 0.2 * kinetic
    velocity = state[1 + axis] * inverse
    flux = [part * velocity for part in state]
    flux[1 + axis] = flux[1 + axis] + pressure
    flux[4] = flux[4] + pressure * velocity
    return flux, jnp.abs(velocity) + jnp.sqrt(1.4 * pressure * inverse)


def shifted_x(own, ghost_low, ghost_high):
    sub = lax.broadcasted_iota(i32, (4, 8, 128), 1)
    down = pltpu.roll(own, 2, 1)
    entering = pltpu.roll(ghost_low[3], 2, 0)
    low = jnp.where(sub < 2, jnp.concatenate([entering[None], down[:3]], axis=0), down)
    up = pltpu.roll(own, 6, 1)
    entering = pltpu.roll(ghost_high[0], 6, 0)
    high = jnp.where(sub >= 6, jnp.concatenate([up[1:], entering[None]], axis=0), up)
    return low, high


def swap_rows(value, odd):
    return jnp.where(odd, pltpu.roll(value, 1, 1), pltpu.roll(value, 7, 1))


def shifted_y(own, ghost_low, ghost_high):
    odd = (lax.broadcasted_iota(i32, (4, 8, 128), 1) & 1) == 1
    lane = lax.broadcasted_iota(i32, (4, 8, 128), 2)
    low = swap_rows(jnp.where(odd, ghost_low, own), odd)
    low = pltpu.roll(jnp.where(lane >= 112, low, own), 16, 2)
    high = swap_rows(jnp.where(odd, own, ghost_high), odd)
    high = pltpu.roll(jnp.where(lane < 16, high, own), 112, 2)
    return low, high


def shifted_z(own, ghost_low, ghost_high):
    z = lax.broadcasted_iota(i32, (4, 8, 128), 2) & 15
    low = jnp.where(z == 0, pltpu.roll(ghost_low, 113, 2), pltpu.roll(own, 1, 2))
    high = jnp.where(z == 15, pltpu.roll(ghost_high, 15, 2), pltpu.roll(own, 127, 2))
    return low, high


def advance_block(source, put, block, ghost_index):
    shape = (4, 8, 128)
    own = [source[block, c].reshape(shape) for c in range(5)]
    inverse = 1.0 / own[0]
    kinetic = (own[1] * own[1] + own[2] * own[2] + own[3] * own[3]) * inverse
    pressure = 0.4 * own[4] - 0.2 * kinetic
    sound = jnp.sqrt(1.4 * pressure * inverse)
    total = [None] * 5
    for axis, shifted in enumerate((shifted_x, shifted_y, shifted_z)):
        low_at = ghost_index[block * 6 + 2 * axis]
        high_at = ghost_index[block * 6 + 2 * axis + 1]
        low, high = [], []
        for c in range(5):
            below, above = shifted(
                own[c], source[low_at, c].reshape(shape), source[high_at, c].reshape(shape)
            )
            low.append(below)
            high.append(above)
        speed = jnp.abs(own[1 + axis] * inverse) + sound
        low_flux, low_speed = flux_and_speed(low, axis)
        high_flux, high_speed = flux_and_speed(high, axis)
        low_speed = jnp.maximum(low_speed, speed)
        high_speed = jnp.maximum(high_speed, speed)
        for c in range(5):
            part = high_flux[c] - low_flux[c]
            part = part + low_speed * (own[c] - low[c]) - high_speed * (high[c] - own[c])
            total[c] = part if axis == 0 else total[c] + part
    for c in range(5):
        put(block, c, (own[c] - 0.04 * total[c]).reshape(32, 128))


def kernel(
    sizes,
    send_left,
    send_right,
    new_source,
    face_source,
    request_slot,
    request_code,
    fine_hbm,
    old_hbm,
    new_hbm,
    flux_hbm,
    fine_out,
    coarse_out,
    fine_in,
    old_in,
    new_in,
    flux_in,
    codes_out,
    codes_in,
    codes_at,
    wants_out,
    wants_in,
    wants_at,
    ghost_index,
    face_at,
    slot_from,
    face_want,
    own_rows,
    made_rows,
    table_rows,
    own_flat,
    pool,
    moved,
    bundle,
    table,
    payload_out,
    payload_in,
    state_a,
    state_b,
    state_c,
    pick_index,
    pick_mask,
    spread_index,
    grow_index,
    faces_out_a,
    faces_out_b,
    faces_in_a,
    faces_in_b,
    edge_own,
    edge_coarse,
    register,
    average,
    parcel_out,
    parcel_in,
    gathered,
    code_rows,
    load_sem,
    local_sem,
    code_send,
    code_recv,
    want_send,
    want_recv,
    block_send,
    block_recv,
    payload_send,
    payload_recv,
    face_send,
    face_recv,
    parcel_send,
    parcel_recv,
):
    n_gx, n_gy, n_gz = sizes
    peers = n_gy * n_gz
    ranks = n_gx * peers
    gx, gy, gz = lax.axis_index("gx"), lax.axis_index("gy"), lax.axis_index("gz")
    me = gy * n_gz + gz
    rank = gx * peers + me

    at_y = [gy] + [lax.rem(gy + step, n_gy) for step in range(1, n_gy)]
    at_z = [gz] + [lax.rem(gz + step, n_gz) for step in range(1, n_gz)]

    def peer_at(step):
        y, z = at_y[step // n_gz], at_z[step % n_gz]
        return y * n_gz + z, (gx, y, z)

    def on_curve(index):
        return (lax.div(index, peers), lax.rem(lax.div(index, n_gz), n_gy), lax.rem(index, n_gz))

    beside = (on_curve(lax.rem(rank + ranks - 1, ranks)), on_curve(lax.rem(rank + 1, ranks)))

    faces_out, faces_in = (faces_out_a, faces_out_b), (faces_in_a, faces_in_b)
    barrier = pltpu.get_barrier_semaphore()

    def greet(step):
        pl.semaphore_signal(barrier, inc=1, device_id=peer_at(step + 1)[1], device_id_type=MESH)

    for step in range(peers - 1):
        greet(step)
    for device in beside:
        pl.semaphore_signal(barrier, inc=1, device_id=device, device_id_type=MESH)

    loads = [
        pltpu.make_async_copy(fine_hbm, fine_in, load_sem.at[0]),
        pltpu.make_async_copy(old_hbm, old_in, load_sem.at[1]),
        pltpu.make_async_copy(new_hbm, new_in, load_sem.at[2]),
        pltpu.make_async_copy(flux_hbm, flux_in, load_sem.at[3]),
    ]
    for load in loads:
        load.start()

    lane1 = lane_of(1)
    place_of = lax.broadcasted_iota(i32, (peers, 128), 0) * CAP + lane_of(peers)
    rows = jnp.full((peers, 128), -1, i32)
    for r in range(REQ):
        rows = jnp.where(place_of == request_slot[r], request_code[r], rows)
    code_rows[...] = jnp.where(lane_of(peers) < CAP, rows, -1)
    for peer in range(peers):
        codes_out[peer] = code_rows[pl.ds(peer, 1), :]

    pl.semaphore_wait(barrier, peers + 1)

    def code_copy(step):
        index, device = peer_at(step)
        return pltpu.make_async_remote_copy(
            src_ref=codes_out.at[index],
            dst_ref=codes_in.at[me],
            send_sem=code_send.at[step],
            recv_sem=code_recv.at[step],
            device_id=device,
            device_id_type=MESH,
        )

    def start_codes(step):
        code_copy(step + 1).start()

    for step in range(peers - 1):
        start_codes(step)

    def rows_of(block, c):
        return pl.ds(pl.multiple_of((block * 5 + c) * 32, 32), 32)

    loads[0].wait()

    def unfold(i):
        c, k = lax.div(i, 32), lax.rem(i, 32)
        value = fine_in[c, :, pl.ds(pl.multiple_of(k * 128, 128), 128)]
        own_rows[pl.ds(i, SLOTS, stride=160), :] = value

    loop(160, unfold, 16)

    def split_own(block):
        for c in range(5):
            value = own_rows[rows_of(block, c), :]
            own_flat[block, c] = value
            pool[block, c] = value

    loop(SLOTS, split_own, 2)
    for side, listed in enumerate((send_left, send_right)):
        for j in range(2):
            bundle[side, j] = own_flat[listed[j]]

    def beside_copy(side, source, target, send, recv):
        return pltpu.make_async_remote_copy(
            src_ref=source,
            dst_ref=target,
            send_sem=send,
            recv_sem=recv,
            device_id=beside[side],
            device_id_type=MESH,
        )

    block_copies = [
        beside_copy(
            side,
            bundle.at[side],
            moved.at[1 - side],
            block_send.at[side],
            block_recv.at[1 - side],
        )
        for side in range(2)
    ]
    for copy in block_copies:
        copy.start()

    loads[1].wait()
    loads[2].wait()
    lane8, lane4 = lane_of(8), lane_of(4)

    def both(c, k):
        at = pl.ds(k * 128, 128)
        return old_in[c, :, at], new_in[c, :, at]

    def put_face(c, face, quadrant, value):
        table_rows[pl.ds((face * 4 + quadrant) * 8 + c, CSLOTS, stride=24 * 8), :] = value

    def fill_table(c):
        for side in range(2):
            for half in range(2):
                first, second = both(c, 30 * side + half)
                for low, value in enumerate(merge_halves(first, second, 4)):
                    put_face(c, side, half * 2 + low, value)
        for side in range(2):

            def fill_y(half, side=side):
                rows = jnp.zeros((8, 128), f32)
                for x in range(8):
                    value = jnp.concatenate(both(c, half * 16 + 2 * x + side), axis=0)
                    shift = (16 * x - 112 * side) % 128
                    value = value if shift == 0 else pltpu.roll(value, shift, 1)
                    rows = jnp.where((lane8 >> 4) == x, value, rows)
                for low, value in enumerate(merge_halves(rows[:4], rows[4:], 4)):
                    put_face(c, 2 + side, half * 2 + low, value)

            for half in range(2):
                fill_y(half)

            def fill_z(quadrant, side=side):
                rows = jnp.zeros((8, 128), f32)
                index = (lane8 & 7) * 16 + 15 * side
                for x in range(8):
                    k = (quadrant // 2) * 16 + 2 * x + quadrant % 2
                    value = pick(jnp.concatenate(both(c, k), axis=0), index)
                    rows = jnp.where((lane8 >> 4) == x, value, rows)
                put_face(c, 4 + side, quadrant, jnp.where((lane4 & 15) < 8, rows[:4], rows[4:]))

            for quadrant in range(4):
                fill_z(quadrant)

        def fill_octant(i):
            half, pair = i // 8, i % 8
            at = (4 * pair + half) * 128
            first = old_in[c, :, pl.ds(at, 128)]
            second = old_in[c, :, pl.ds(at + 256, 128)]
            for low, value in enumerate(merge_halves(first, second, 4)):
                code = 96 + ((pair // 4) * 4 + half * 2 + low) * 4 + pair % 4
                table_rows[pl.ds(code * 8 + c, CSLOTS, stride=32 * 8), :] = value

        for i in range(16):
            fill_octant(i)

    loop(5, fill_table)

    def split_table(code):
        table[code] = table_rows[pl.ds(pl.multiple_of(code * 8, 8), 8), :]

    loop(224, split_table, 16)

    def wait_codes(step):
        code_copy(step + 1).wait_recv()

    for step in range(peers - 1):
        wait_codes(step)
    codes_in[me] = codes_out[me]
    to_scalars = pltpu.make_async_copy(codes_in, codes_at, local_sem.at[0])
    to_scalars.start()
    to_scalars.wait()

    def answer(peer, place):
        code = jnp.maximum(codes_at[peer, 0, place], 0)
        return table[code][:5]

    def payload_copy(step):
        index, device = peer_at(step)
        return pltpu.make_async_remote_copy(
            src_ref=payload_out.at[pl.ds(step * CAP, CAP)],
            dst_ref=payload_in.at[pl.ds(me * CAP, CAP)],
            send_sem=payload_send.at[step],
            recv_sem=payload_recv.at[step],
            device_id=device,
            device_id_type=MESH,
        )

    for first in range(1, peers, 8):
        group = range(first, min(first + 8, peers))
        for step in group:
            index, _ = peer_at(step)
            for place in range(CAP):
                payload_out[step * CAP + place] = answer(index, place)
        for step in group:
            payload_copy(step).start()
    for step in range(1, peers):
        code_copy(step).wait_send()

    def scan(i, carry):
        count, wants, places = carry
        e = face_source[lax.div(i, 6), lax.rem(i, 6)]
        is_left = e < FACES
        is_right = (e >= 2 * FACES) & (e < 3 * FACES)
        index = jnp.where(
            is_left,
            SLOTS + jnp.minimum(count[0], 2),
            jnp.where(
                is_right,
                SLOTS + 3 + jnp.minimum(count[1], 2),
                jnp.where(e >= 3 * FACES, SLOTS + 6 + e - 3 * FACES, lax.div(jnp.maximum(e - FACES, 0), 6)),
            ),
        )
        ghost_index[i] = index
        new_wants = tuple(
            jnp.where(is_left & (count[0] == j), e, wants[j]) for j in range(3)
        ) + tuple(
            jnp.where(is_right & (count[1] == j), e - 2 * FACES, wants[3 + j]) for j in range(3)
        )
        new_places = tuple(
            jnp.where(e == 3 * FACES + r, i, places[r]) for r in range(FACEREQ)
        )
        new_count = (
            count[0] + jnp.where(is_left, 1, 0),
            count[1] + jnp.where(is_right, 1, 0),
        )
        return new_count, new_wants, new_places

    zero = jnp.int32(0)
    _, wants, places = lax.fori_loop(
        0, FACES, scan, ((zero, zero), (zero,) * 6, (zero,) * FACEREQ)
    )
    for r in range(FACEREQ):
        face_at[r] = places[r]
    for side in range(2):
        row = jnp.zeros((1, 128), i32)
        for j in range(3):
            row = jnp.where(lane1 == j, wants[3 * side + j], row)
        wants_out[side] = row

    def invert(slot):
        found = jnp.int32(0)
        for r in range(FACEREQ):
            found = jnp.where(request_slot[r] == slot, r, found)
        slot_from[slot] = found

    want_copies = [
        beside_copy(
            side, wants_out.at[side], wants_in.at[1 - side], want_send.at[side], want_recv.at[1 - side]
        )
        for side in range(2)
    ]
    for copy in want_copies:
        copy.start()
    sub = lax.broadcasted_iota(i32, (32, 128), 0)
    lane = lax.broadcasted_iota(i32, (32, 128), 1)
    x, yh = sub >> 1, sub & 1
    for face in range(6):
        axis, side = face // 2, face % 2
        if axis == 0:
            pick_index[face] = lane8
        elif axis == 1:
            pick_index[face] = 112 * side + (lane8 & 15)
        else:
            pick_index[face] = (lane8 & 7) * 16 + 15 * side
        for half in range(2):
            if axis == 0:
                mask = sub == 30 * side + half
            else:
                mask = ((x >> 3) == half) & ((lane >> 4) == (x & 7))
                if axis == 1:
                    mask = mask & (yh == side)
                else:
                    mask = mask & (((lane >> 3) & 1) == yh)
            pick_mask[face, half] = jnp.where(mask, 1.0, 0.0)
    spread_index[0] = lane
    spread_index[1] = (x & 7) * 16 + (lane & 15)
    spread_index[2] = (x & 7) * 16 + 8 * yh + (lane >> 4)
    grow_index[0] = (4 * yh + (lane >> 5)) * 16 + ((lane & 15) >> 1)
    grow_index[1] = (x >> 1) * 16 + ((lane & 15) >> 1)
    grow_index[2] = (x >> 1) * 16 + 4 * yh + (lane >> 5)

    loop(peers * CAP, invert, 8)

    for copy in want_copies:
        copy.wait()
    to_scalars = pltpu.make_async_copy(wants_in, wants_at, local_sem.at[1])
    to_scalars.start()
    to_scalars.wait()
    for peer in range(peers):
        code_rows[pl.ds(peer, 1), :] = codes_in[peer]
    for copy in block_copies:
        copy.wait()
    for side in range(2):
        for j in range(2):
            pool[SLOTS + 2 * side + j] = moved[side, j]

    def wait_payload(step):
        payload_copy(step + 1).wait_recv()

    for step in range(peers - 1):
        wait_payload(step)
    for place in range(CAP):
        payload_in[me * CAP + place] = answer(me, place)

    lane5 = lane_of(5)
    grow5 = [(4 * half + (lane5 >> 5)) * 16 + ((lane5 & 15) >> 1) for half in range(2)]
    for block in range(NEWB):
        for piece in range(OCTP):
            value = payload_in[request_slot[FACEREQ + block * OCTP + piece]]
            for part in range(2):
                for half in range(2):
                    grown = pick(value, grow5[half] + 8 * part)
                    for twin in range(2):
                        k = 2 * (4 * piece + 2 * part + twin) + half
                        made_rows[pl.ds(block * 160 + k, 5, stride=32), :] = grown

    for block in range(NEWB):
        for c in range(5):
            pool[10 + block, c] = made_rows[rows_of(block, c), :]

    def regrid(block):
        state_a[block] = pool[new_source[block]]

    loop(SLOTS, regrid, 2)

    def take_face(state, face_id, put):
        block, face = lax.div(face_id, 6), lax.rem(face_id, 6)
        index = pick_index[face]
        masks = [pick_mask[face, half].reshape(4, 8, 128) for half in range(2)]
        for c in range(5):
            value = state[block, c].reshape(4, 8, 128)
            picked = [pick(value[v], index) for v in range(4)]
            for half in range(2):
                rows = picked[0] * masks[half][0]
                for v in range(1, 4):
                    rows = rows + picked[v] * masks[half][v]
                put(c, half, jnp.sum(rows, axis=0, keepdims=True))

    def send_faces(step, state):
        def one(i):
            side, j = (i // 3, i % 3) if isinstance(i, int) else (lax.div(i, 3), lax.rem(i, 3))

            def put(c, half, row):
                faces_out[step][side, j, pl.ds(2 * c + half, 1), :] = row

            take_face(state, wants_at[side, 0, j], put)

        loop(6, one, 3)
        copies = [
            beside_copy(
                side,
                faces_out[step].at[side],
                faces_in[step].at[1 - side],
                face_send.at[step, side],
                face_recv.at[step, 1 - side],
            )
            for side in range(2)
        ]
        for copy in copies:
            copy.start()
        return copies

    def take_edges(state):
        def one(r):
            def put(c, half, row):
                edge_own[c, pl.ds(2 * r + half, 1), :] = row

            take_face(state, face_at[r], put)

        loop(FACEREQ, one, 3)

    def place_faces(step, state):
        def one(i):
            side, j = (i // 3, i % 3) if isinstance(i, int) else (lax.div(i, 3), lax.rem(i, 3))
            face = lax.rem(wants_out_face(side, j), 6)
            axis = lax.div(face, 2)
            index = spread_index[axis].reshape(4, 8, 128)
            odd = (lax.broadcasted_iota(i32, (8, 128), 0) & 1) == 1
            for c in range(5):
                first = jnp.broadcast_to(faces_in[step][side, j, pl.ds(2 * c, 1), :], (8, 128))
                second = jnp.broadcast_to(faces_in[step][side, j, pl.ds(2 * c + 1, 1), :], (8, 128))
                both_rows = jnp.where(odd, second, first)
                parts = []
                for v in range(4):
                    rows = jnp.where(axis == 0, both_rows, first if v < 2 else second)
                    parts.append(pick(rows, index[v]))
                state[SLOTS + i, c] = jnp.concatenate(parts, axis=0)

        loop(6, one, 3)

    def wants_out_face(side, j):
        return face_want[side * 3 + j]

    for j in range(6):
        face_want[j] = wants[j]

    def register_step(step):
        axis_row = jnp.zeros((16, 128), i32)
        sign_row = jnp.zeros((16, 128), f32)
        row = lax.broadcasted_iota(i32, (16, 128), 0) >> 1
        for r in range(FACEREQ):
            face = lax.rem(face_at[r], 6)
            axis_row = jnp.where(row == r, lax.div(face, 2), axis_row)
            sign_row = jnp.where(row == r, (2 * lax.rem(face, 2) - 1).astype(f32), sign_row)
        is_axis = [axis_row == axis for axis in range(3)]
        own = [edge_own[c] for c in range(5)]
        old = [edge_coarse[0, c] for c in range(5)]
        ghost = old
        if step == 1:
            ghost = [old[c] + 0.5 * (edge_coarse[1, c] - old[c]) for c in range(5)]

        def parts(state):
            inverse = 1.0 / state[0]
            normal = jnp.where(is_axis[0], state[1], jnp.where(is_axis[1], state[2], state[3]))
            kinetic = (state[1] * state[1] + state[2] * state[2] + state[3] * state[3]) * inverse
            pressure = 0.4 * state[4] - 0.2 * kinetic
            velocity = normal * inverse
            flux = [part * velocity for part in state]
            for axis in range(3):
                flux[1 + axis] = flux[1 + axis] + jnp.where(is_axis[axis], pressure, 0.0)
            flux[4] = flux[4] + pressure * velocity
            return flux, jnp.abs(velocity) + jnp.sqrt(1.4 * pressure * inverse)

        own_flux, own_speed = parts(own)
        ghost_flux, ghost_speed = parts(ghost)
        speed = jnp.maximum(own_speed, ghost_speed) * sign_row
        for c in range(5):
            value = 0.5 * (own_flux[c] + ghost_flux[c]) - 0.5 * speed * (ghost[c] - own[c])
            at = pl.ds(16 * c, 16)
            register[at, :] = value if step == 0 else register[at, :] + value

    copies = send_faces(0, state_a)
    edge_own[...] = jnp.ones((5, 16, 128), f32)
    edge_coarse[...] = jnp.ones((2, 5, 16, 128), f32)
    take_edges(state_a)

    def coarse_ghosts(r):
        slot = request_slot[r]
        axis = lax.div(lax.rem(face_at[r], 6), 2)
        index = grow_index[axis].reshape(4, 8, 128)
        value = payload_in[slot]
        for when in range(2):
            for half in range(2):
                grown = pick(value, grow5[half] + 8 * when)
                for c in range(5):
                    edge_coarse[when, c, pl.ds(2 * r + half, 1), :] = grown[c : c + 1]
        for c in range(5):
            rows = jnp.broadcast_to(value[c : c + 1], (8, 128))
            old = jnp.concatenate([pick(rows, index[v]) for v in range(4)], axis=0)
            new = jnp.concatenate([pick(rows, index[v] + 8) for v in range(4)], axis=0)
            state_a[SLOTS + 6 + r, c] = old
            state_b[SLOTS + 6 + r, c] = old + 0.5 * (new - old)

    loop(FACEREQ, coarse_ghosts, 2)
    register_step(0)
    for step in range(1, peers):
        payload_copy(step).wait_send()
    for copy in copies:
        copy.wait()
    place_faces(0, state_a)

    def first_step(block):
        def put(block, c, value):
            state_b[block, c] = value

        advance_block(state_a, put, block, ghost_index)

    loop(SLOTS, first_step)

    copies = send_faces(1, state_b)
    take_edges(state_b)
    register_step(1)

    lane16 = lane_of(16)
    shrink = ((lane16 >> 4) & 3) * 32 + 2 * (lane16 & 7)
    for c in range(5):
        value = register[16 * c : 16 * c + 16, :]
        value = value + pltpu.roll(value, 127, 1)
        value = value + pltpu.roll(value, 112, 1)
        value = value * 0.125
        register[16 * c : 16 * c + 16, :] = jnp.concatenate(
            [pick(value[:8], shrink[:8]), pick(value[8:], shrink[8:])], axis=0
        )
    for r in range(FACEREQ):
        first = register[pl.ds(2 * r, 5, stride=16), :]
        second = register[pl.ds(2 * r + 1, 5, stride=16), :]
        average[r] = jnp.where(lane5 < 64, first, second)

    def parcel_copy(step):
        index, device = peer_at(step)
        return pltpu.make_async_remote_copy(
            src_ref=parcel_out.at[pl.ds(step * 2, 2)],
            dst_ref=parcel_in.at[pl.ds(me * 2, 2)],
            send_sem=parcel_send.at[step],
            recv_sem=parcel_recv.at[step],
            device_id=device,
            device_id_type=MESH,
        )

    def parcel(row):
        first = average[slot_from[2 * row]]
        second = average[slot_from[2 * row + 1]]
        return jnp.where((lane5 & 15) < 8, first, second)

    for first in range(1, peers, 8):
        group = range(first, min(first + 8, peers))
        for step in group:
            index, _ = peer_at(step)
            for pair in range(2):
                parcel_out[step * 2 + pair] = parcel(index * 2 + pair)
        for step in group:
            parcel_copy(step).start()

    for copy in copies:
        copy.wait()
    place_faces(1, state_b)

    def second_step(block):
        def put(block, c, value):
            state_c[rows_of(block, c), :] = value

        advance_block(state_b, put, block, ghost_index)

    loop(SLOTS, second_step)

    def fold(i):
        c, k = lax.div(i, 32), lax.rem(i, 32)
        value = state_c[pl.ds(i, SLOTS, stride=160), :]
        fine_out[c, :, pl.ds(pl.multiple_of(k * 128, 128), 128)] = value

    loop(160, fold, 16)

    target = lax.broadcasted_iota(i32, (peers, 128), 1)
    wanted = jnp.where(target < 24 * CSLOTS, (target & 3) * 24 + (target >> 2), -7)
    chosen = []
    for half in range(2):
        picks = [
            (jnp.broadcast_to(code_rows[:, 2 * pair + half : 2 * pair + half + 1], (peers, 128)) == wanted)
            for pair in range(2)
        ]
        chosen.append(
            jnp.concatenate([jnp.where(p, 1.0, 0.0) for p in picks], axis=0).astype(jnp.bfloat16)
        )

    def contract(left, right):
        return lax.dot_general(
            left, right, (((0,), (0,)), ((), ())), preferred_element_type=f32
        )

    ones = jnp.ones((2 * peers, 128), jnp.bfloat16)
    counts = contract(chosen[0], ones) + contract(chosen[1], ones)
    loads[3].wait()

    def wait_parcel(step):
        parcel_copy(step + 1).wait()

    for step in range(peers - 1):
        wait_parcel(step)
    for pair in range(2):
        parcel_in[me * 2 + pair] = parcel(me * 2 + pair)

    def line_up(peer):
        for pair in range(2):
            gathered[pl.ds(pair * peers + peer, 5, stride=2 * peers), :] = parcel_in[peer * 2 + pair]

    loop(peers, line_up, 8)
    low8, low4 = (lane8 & 15) < 8, (lane4 & 15) < 8
    for c in range(5):
        value = gathered[pl.ds(c * 2 * peers, 2 * peers), :]
        coarse_part = value.astype(jnp.bfloat16)
        rest = (value - coarse_part.astype(f32)).astype(jnp.bfloat16)
        sums = [contract(chosen[h], coarse_part) + contract(chosen[h], rest) for h in range(2)]
        change = {}
        for face in range(6):
            scale = 0.08 if face % 2 else -0.08
            for half in range(2):
                at = (face * 2 + half) * 8
                first, second = sums[0][at : at + 8], sums[1][at : at + 8]
                count = counts[at : at + 8]
                lows = first + pltpu.roll(second, 120, 1)
                highs = second + pltpu.roll(first, 8, 1)
                total = jnp.where(low4, lows[:4], highs[4:])
                number = jnp.where(low4, count[:4], count[4:])
                flux = flux_in[face, c, :, pl.ds(half * 128, 128)]
                change[face, half] = scale * (number * flux - total)
        stacked = {
            face: jnp.concatenate([change[face, 0], change[face, 1]], axis=0) for face in range(2, 6)
        }
        for x8 in range(8):
            for yh8 in range(2):
                shift = (112 * yh8 - 16 * x8) % 128
                moved = stacked[2 + yh8]
                moved = moved if shift == 0 else pltpu.roll(moved, shift, 1)
                added = jnp.where((lane8 >> 4) == 7 * yh8, moved, 0.0)
                index = x8 * 16 + 8 * yh8 + (lane8 >> 4)
                added = added + jnp.where((lane8 & 15) == 0, pick(stacked[4], index), 0.0)
                added = added + jnp.where((lane8 & 15) == 15, pick(stacked[5], index), 0.0)
                for upper in range(2):
                    x_at = 8 * upper + x8
                    at = pl.ds((2 * x_at + yh8) * 128, 128)
                    value = new_in[c, :, at] + added[4 * upper : 4 * upper + 4]
                    if x_at == 0:
                        value = value + change[0, yh8]
                    if x_at == 15:
                        value = value + change[1, yh8]
                    coarse_out[c, :, at] = value


def on_device(sizes, fine_old, send_left, send_right, new_source, face_source, request_slot, request_code,
              coarse_old, coarse_new, coarse_flux):
    peers = sizes[1] * sizes[2]
    smem = pl.BlockSpec(memory_space=pltpu.SMEM)
    vmem = pl.BlockSpec(memory_space=pltpu.VMEM)
    hbm = pl.BlockSpec(memory_space=pltpu.HBM)
    dma = pltpu.SemaphoreType.DMA
    V = pltpu.VMEM
    fine, coarse = pl.pallas_call(
        functools.partial(kernel, sizes),
        out_shape=(
            jax.ShapeDtypeStruct((5, SLOTS, 4096), f32),
            jax.ShapeDtypeStruct((5, CSLOTS, 4096), f32),
        ),
        in_specs=[smem] * 6 + [hbm] * 4,
        out_specs=(vmem, vmem),
        scratch_shapes=[
            V((5, SLOTS, 4096), f32),
            V((5, CSLOTS, 4096), f32),
            V((5, CSLOTS, 4096), f32),
            V((6, 5, CSLOTS, 256), f32),
            V((peers, 1, 128), i32),
            V((peers, 1, 128), i32),
            pltpu.SMEM((peers, 1, 128), i32),
            V((2, 1, 128), i32),
            V((2, 1, 128), i32),
            pltpu.SMEM((2, 1, 128), i32),
            pltpu.SMEM((FACES,), i32),
            pltpu.SMEM((8,), i32),
            pltpu.SMEM((peers * CAP,), i32),
            pltpu.SMEM((8,), i32),
            V((8 * 160, 128), f32),
            V((416, 128), f32),
            V((2816, 128), f32),
            V((SLOTS, 5, 32, 128), f32),
            V((12, 5, 32, 128), f32),
            V((2, 2, 5, 32, 128), f32),
            V((2, 2, 5, 32, 128), f32),
            V((224, 8, 128), f32),
            V((peers * CAP, 5, 128), f32),
            V((peers * CAP, 5, 128), f32),
            V((18, 5, 32, 128), f32),
            V((18, 5, 32, 128), f32),
            V((8 * 160, 128), f32),
            V((6, 8, 128), i32),
            V((6, 2, 32, 128), f32),
            V((3, 32, 128), i32),
            V((3, 32, 128), i32),
            V((2, 3, 10, 128), f32),
            V((2, 3, 10, 128), f32),
            V((2, 3, 10, 128), f32),
            V((2, 3, 10, 128), f32),
            V((5, 16, 128), f32),
            V((2, 5, 16, 128), f32),
            V((128, 128), f32),
            V((FACEREQ, 5, 128), f32),
            V((peers * 2, 5, 128), f32),
            V((peers * 2, 5, 128), f32),
            V((8 * 2 * peers, 128), f32),
            V((peers, 128), i32),
            dma((4,)),
            dma((2,)),
            dma((peers,)),
            dma((peers,)),
            dma((2,)),
            dma((2,)),
            dma((2,)),
            dma((2,)),
            dma((peers,)),
            dma((peers,)),
            dma((2, 2)),
            dma((2, 2)),
            dma((peers,)),
            dma((peers,)),
        ],
        compiler_params=pltpu.CompilerParams(
            collective_id=0, has_side_effects=True, vmem_limit_bytes=64 * 1024 * 1024
        ),
    )(
        send_left,
        send_right,
        new_source,
        face_source,
        request_slot,
        request_code,
        jnp.transpose(fine_old, (1, 0, 2)),
        jnp.transpose(coarse_old, (1, 0, 2)),
        jnp.transpose(coarse_new, (1, 0, 2)),
        jnp.transpose(coarse_flux, (1, 2, 0, 3)),
    )
    return jnp.transpose(fine, (1, 0, 2)), jnp.transpose(coarse, (1, 0, 2))


def solution(mesh):
    sizes = (mesh.shape["gx"], mesh.shape["gy"], mesh.shape["gz"])
    every = ("gx", "gy", "gz")
    in_specs = (
        P(every, None, None),
        P(every),
        P(every),
        P(every),
        P(every, None),
        P(every),
        P(every),
        P(every, None, None),
        P(every, None, None),
        P(every, None, None, None),
    )
    out_specs = (P(every, None, None), P(every, None, None))
    return jax.shard_map(
        functools.partial(on_device, sizes), mesh=mesh, in_specs=in_specs, out_specs=out_specs, check_vma=False
    )
```

```python
import functools

import jax
import jax.numpy as jnp
from jax import lax
from jax.experimental import pallas as pl
from jax.experimental.pallas import tpu as pltpu
from jax.sharding import PartitionSpec as P

MESH = pl.DeviceIdType.MESH
SLOTS = 6
CSLOTS = 4
CAP = 4
FACES = 36
FACEREQ = 6
REQ = 14
NEWB = 2
OCTP = 4
f32 = jnp.float32
i32 = jnp.int32


def pick(x, idx):
    return jnp.take_along_axis(x, idx, axis=1, mode="promise_in_bounds")


def loop(count, body, unroll=1):
    def step(i, carry):
        for part in range(unroll):
            body(i * unroll + part)
        return carry

    lax.fori_loop(0, count // unroll, step, 0)
    for i in range(count - count % unroll, count):
        body(i)


def lane_of(rows):
    return lax.broadcasted_iota(i32, (rows, 128), 1)


def merge_halves(first, second, rows):
    low = (lane_of(rows) & 15) < 8
    return (
        jnp.where(low, first, pltpu.roll(second, 8, 1)),
        jnp.where(low, pltpu.roll(first, 120, 1), second),
    )


def flux_and_speed(state, axis):
    density, energy = state[0], state[4]
    inverse = 1.0 / density
    kinetic = (state[1] * state[1] + state[2] * state[2] + state[3] * state[3]) * inverse
    pressure = 0.4 * energy - 0.2 * kinetic
    velocity = state[1 + axis] * inverse
    flux = [part * velocity for part in state]
    flux[1 + axis] = flux[1 + axis] + pressure
    flux[4] = flux[4] + pressure * velocity
    return flux, jnp.abs(velocity) + jnp.sqrt(1.4 * pressure * inverse)


def shifted_x(own, ghost_low, ghost_high):
    sub = lax.broadcasted_iota(i32, (4, 8, 128), 1)
    down = pltpu.roll(own, 2, 1)
    entering = pltpu.roll(ghost_low[3], 2, 0)
    low = jnp.where(sub < 2, jnp.concatenate([entering[None], down[:3]], axis=0), down)
    up = pltpu.roll(own, 6, 1)
    entering = pltpu.roll(ghost_high[0], 6, 0)
    high = jnp.where(sub >= 6, jnp.concatenate([up[1:], entering[None]], axis=0), up)
    return low, high


def swap_rows(value, odd):
    return jnp.where(odd, pltpu.roll(value, 1, 1), pltpu.roll(value, 7, 1))


def shifted_y(own, ghost_low, ghost_high):
    odd = (lax.broadcasted_iota(i32, (4, 8, 128), 1) & 1) == 1
    lane = lax.broadcasted_iota(i32, (4, 8, 128), 2)
    low = swap_rows(jnp.where(odd, ghost_low, own), odd)
    low = pltpu.roll(jnp.where(lane >= 112, low, own), 16, 2)
    high = swap_rows(jnp.where(odd, own, ghost_high), odd)
    high = pltpu.roll(jnp.where(lane < 16, high, own), 112, 2)
    return low, high


def shifted_z(own, ghost_low, ghost_high):
    z = lax.broadcasted_iota(i32, (4, 8, 128), 2) & 15
    low = jnp.where(z == 0, pltpu.roll(ghost_low, 113, 2), pltpu.roll(own, 1, 2))
    high = jnp.where(z == 15, pltpu.roll(ghost_high, 15, 2), pltpu.roll(own, 127, 2))
    return low, high


def advance_block(source, put, block, ghost_index):
    shape = (4, 8, 128)
    own = [source[block, c].reshape(shape) for c in range(5)]
    inverse = 1.0 / own[0]
    kinetic = (own[1] * own[1] + own[2] * own[2] + own[3] * own[3]) * inverse
    pressure = 0.4 * own[4] - 0.2 * kinetic
    sound = jnp.sqrt(1.4 * pressure * inverse)
    total = [None] * 5
    for axis, shifted in enumerate((shifted_x, shifted_y, shifted_z)):
        low_at = ghost_index[block * 6 + 2 * axis]
        high_at = ghost_index[block * 6 + 2 * axis + 1]
        low, high = [], []
        for c in range(5):
            below, above = shifted(
                own[c], source[low_at, c].reshape(shape), source[high_at, c].reshape(shape)
            )
            low.append(below)
            high.append(above)
        speed = jnp.abs(own[1 + axis] * inverse) + sound
        low_flux, low_speed = flux_and_speed(low, axis)
        high_flux, high_speed = flux_and_speed(high, axis)
        low_speed = jnp.maximum(low_speed, speed)
        high_speed = jnp.maximum(high_speed, speed)
        for c in range(5):
            part = high_flux[c] - low_flux[c]
            part = part + low_speed * (own[c] - low[c]) - high_speed * (high[c] - own[c])
            total[c] = part if axis == 0 else total[c] + part
    for c in range(5):
        put(block, c, (own[c] - 0.04 * total[c]).reshape(32, 128))


def kernel(
    sizes,
    send_left,
    send_right,
    new_source,
    face_source,
    request_slot,
    request_code,
    fine_hbm,
    old_hbm,
    new_hbm,
    flux_hbm,
    fine_hand,
    coarse_hand,
    fine_in,
    old_in,
    new_in,
    flux_in,
    codes_out,
    codes_in,
    codes_at,
    wants_out,
    wants_in,
    wants_at,
    ghost_index,
    face_at,
    slot_from,
    face_want,
    own_rows,
    made_rows,
    table_rows,
    own_flat,
    pool,
    moved,
    bundle,
    table,
    payload_out,
    payload_in,
    state_a,
    state_b,
    state_c,
    pick_index,
    pick_mask,
    spread_index,
    grow_index,
    faces_out_a,
    faces_out_b,
    faces_in_a,
    faces_in_b,
    edge_own,
    edge_coarse,
    register,
    average,
    parcel_out,
    parcel_in,
    gathered,
    code_rows,
    fine_out,
    coarse_out,
    store_sem,
    load_sem,
    local_sem,
    code_send,
    code_recv,
    want_send,
    want_recv,
    block_send,
    block_recv,
    payload_send,
    payload_recv,
    face_send,
    face_recv,
    parcel_send,
    parcel_recv,
):
    n_gx, n_gy, n_gz = sizes
    peers = n_gy * n_gz
    ranks = n_gx * peers
    gx, gy, gz = lax.axis_index("gx"), lax.axis_index("gy"), lax.axis_index("gz")
    me = gy * n_gz + gz
    rank = gx * peers + me

    at_y = [gy] + [lax.rem(gy + step, n_gy) for step in range(1, n_gy)]
    at_z = [gz] + [lax.rem(gz + step, n_gz) for step in range(1, n_gz)]

    def peer_at(step):
        y, z = at_y[step // n_gz], at_z[step % n_gz]
        return y * n_gz + z, (gx, y, z)

    def on_curve(index):
        return (lax.div(index, peers), lax.rem(lax.div(index, n_gz), n_gy), lax.rem(index, n_gz))

    beside = (on_curve(lax.rem(rank + ranks - 1, ranks)), on_curve(lax.rem(rank + 1, ranks)))

    faces_out, faces_in = (faces_out_a, faces_out_b), (faces_in_a, faces_in_b)
    barrier = pltpu.get_barrier_semaphore()

    def greet(step):
        pl.semaphore_signal(barrier, inc=1, device_id=peer_at(step + 1)[1], device_id_type=MESH)

    for step in range(peers - 1):
        greet(step)
    for device in beside:
        pl.semaphore_signal(barrier, inc=1, device_id=device, device_id_type=MESH)

    loads = [
        pltpu.make_async_copy(fine_hbm, fine_in, load_sem.at[0]),
        pltpu.make_async_copy(old_hbm, old_in, load_sem.at[1]),
        pltpu.make_async_copy(new_hbm, new_in, load_sem.at[2]),
        pltpu.make_async_copy(flux_hbm, flux_in, load_sem.at[3]),
    ]
    for load in loads:
        load.start()

    lane1 = lane_of(1)
    place_of = lax.broadcasted_iota(i32, (peers, 128), 0) * CAP + lane_of(peers)
    rows = jnp.full((peers, 128), -1, i32)
    for r in range(REQ):
        rows = jnp.where(place_of == request_slot[r], request_code[r], rows)
    code_rows[...] = jnp.where(lane_of(peers) < CAP, rows, -1)
    for peer in range(peers):
        codes_out[peer] = code_rows[pl.ds(peer, 1), :]

    def rows_of(block, c):
        return pl.ds(pl.multiple_of((block * 5 + c) * 32, 32), 32)

    loads[0].wait()

    def unfold(i):
        c, k = lax.div(i, 32), lax.rem(i, 32)
        value = fine_in[c, :, pl.ds(pl.multiple_of(k * 128, 128), 128)]
        own_rows[pl.ds(i, SLOTS, stride=160), :] = value

    loop(160, unfold, 16)

    def split_own(block):
        for c in range(5):
            value = own_rows[rows_of(block, c), :]
            own_flat[block, c] = value
            pool[block, c] = value

    loop(SLOTS, split_own, 2)
    for side, listed in enumerate((send_left, send_right)):
        for j in range(2):
            bundle[side, j] = own_flat[listed[j]]

    loads[1].wait()
    loads[2].wait()
    lane8, lane4 = lane_of(8), lane_of(4)

    def both(c, k):
        at = pl.ds(k * 128, 128)
        return old_in[c, :, at], new_in[c, :, at]

    def put_face(c, face, quadrant, value):
        table_rows[pl.ds((face * 4 + quadrant) * 8 + c, CSLOTS, stride=24 * 8), :] = value

    def fill_table(c):
        for side in range(2):
            for half in range(2):
                first, second = both(c, 30 * side + half)
                for low, value in enumerate(merge_halves(first, second, 4)):
                    put_face(c, side, half * 2 + low, value)
        for side in range(2):

            def fill_y(half, side=side):
                rows = jnp.zeros((8, 128), f32)
                for x in range(8):
                    value = jnp.concatenate(both(c, half * 16 + 2 * x + side), axis=0)
                    shift = (16 * x - 112 * side) % 128
                    value = value if shift == 0 else pltpu.roll(value, shift, 1)
                    rows = jnp.where((lane8 >> 4) == x, value, rows)
                for low, value in enumerate(merge_halves(rows[:4], rows[4:], 4)):
                    put_face(c, 2 + side, half * 2 + low, value)

            for half in range(2):
                fill_y(half)

            def fill_z(quadrant, side=side):
                rows = jnp.zeros((8, 128), f32)
                index = (lane8 & 7) * 16 + 15 * side
                for x in range(8):
                    k = (quadrant // 2) * 16 + 2 * x + quadrant % 2
                    value = pick(jnp.concatenate(both(c, k), axis=0), index)
                    rows = jnp.where((lane8 >> 4) == x, value, rows)
                put_face(c, 4 + side, quadrant, jnp.where((lane4 & 15) < 8, rows[:4], rows[4:]))

            for quadrant in range(4):
                fill_z(quadrant)

        def fill_octant(i):
            half, pair = i // 8, i % 8
            at = (4 * pair + half) * 128
            first = old_in[c, :, pl.ds(at, 128)]
            second = old_in[c, :, pl.ds(at + 256, 128)]
            for low, value in enumerate(merge_halves(first, second, 4)):
                code = 96 + ((pair // 4) * 4 + half * 2 + low) * 4 + pair % 4
                table_rows[pl.ds(code * 8 + c, CSLOTS, stride=32 * 8), :] = value

        for i in range(16):
            fill_octant(i)

    loop(5, fill_table)

    def split_table(code):
        table[code] = table_rows[pl.ds(pl.multiple_of(code * 8, 8), 8), :]

    loop(224, split_table, 16)
    pl.semaphore_wait(barrier, peers + 1)

    def code_copy(step):
        index, device = peer_at(step)
        return pltpu.make_async_remote_copy(
            src_ref=codes_out.at[index],
            dst_ref=codes_in.at[me],
            send_sem=code_send.at[step],
            recv_sem=code_recv.at[step],
            device_id=device,
            device_id_type=MESH,
        )

    def start_codes(step):
        code_copy(step + 1).start()

    for step in range(peers - 1):
        start_codes(step)

    def beside_copy(side, source, target, send, recv):
        return pltpu.make_async_remote_copy(
            src_ref=source,
            dst_ref=target,
            send_sem=send,
            recv_sem=recv,
            device_id=beside[side],
            device_id_type=MESH,
        )

    block_copies = [
        beside_copy(
            side,
            bundle.at[side],
            moved.at[1 - side],
            block_send.at[side],
            block_recv.at[1 - side],
        )
        for side in range(2)
    ]
    for copy in block_copies:
        copy.start()


    def wait_codes(step):
        code_copy(step + 1).wait_recv()

    for step in range(peers - 1):
        wait_codes(step)
    codes_in[me] = codes_out[me]
    to_scalars = pltpu.make_async_copy(codes_in, codes_at, local_sem.at[0])
    to_scalars.start()
    to_scalars.wait()

    def answer(peer, place):
        code = jnp.maximum(codes_at[peer, 0, place], 0)
        return table[code][:5]

    def payload_copy(step):
        index, device = peer_at(step)
        return pltpu.make_async_remote_copy(
            src_ref=payload_out.at[pl.ds(step * CAP, CAP)],
            dst_ref=payload_in.at[pl.ds(me * CAP, CAP)],
            send_sem=payload_send.at[step],
            recv_sem=payload_recv.at[step],
            device_id=device,
            device_id_type=MESH,
        )

    for first in range(1, peers, 8):
        group = range(first, min(first + 8, peers))
        for step in group:
            index, _ = peer_at(step)
            for place in range(CAP):
                payload_out[step * CAP + place] = answer(index, place)
        for step in group:
            payload_copy(step).start()
    for step in range(1, peers):
        code_copy(step).wait_send()

    def scan(i, carry):
        count, wants, places = carry
        e = face_source[lax.div(i, 6), lax.rem(i, 6)]
        is_left = e < FACES
        is_right = (e >= 2 * FACES) & (e < 3 * FACES)
        index = jnp.where(
            is_left,
            SLOTS + jnp.minimum(count[0], 2),
            jnp.where(
                is_right,
                SLOTS + 3 + jnp.minimum(count[1], 2),
                jnp.where(e >= 3 * FACES, SLOTS + 6 + e - 3 * FACES, lax.div(jnp.maximum(e - FACES, 0), 6)),
            ),
        )
        ghost_index[i] = index
        new_wants = tuple(
            jnp.where(is_left & (count[0] == j), e, wants[j]) for j in range(3)
        ) + tuple(
            jnp.where(is_right & (count[1] == j), e - 2 * FACES, wants[3 + j]) for j in range(3)
        )
        new_places = tuple(
            jnp.where(e == 3 * FACES + r, i, places[r]) for r in range(FACEREQ)
        )
        new_count = (
            count[0] + jnp.where(is_left, 1, 0),
            count[1] + jnp.where(is_right, 1, 0),
        )
        return new_count, new_wants, new_places

    zero = jnp.int32(0)
    _, wants, places = lax.fori_loop(
        0, FACES, scan, ((zero, zero), (zero,) * 6, (zero,) * FACEREQ)
    )
    for r in range(FACEREQ):
        face_at[r] = places[r]
    for side in range(2):
        row = jnp.zeros((1, 128), i32)
        for j in range(3):
            row = jnp.where(lane1 == j, wants[3 * side + j], row)
        wants_out[side] = row

    def invert(slot):
        found = jnp.int32(0)
        for r in range(FACEREQ):
            found = jnp.where(request_slot[r] == slot, r, found)
        slot_from[slot] = found

    want_copies = [
        beside_copy(
            side, wants_out.at[side], wants_in.at[1 - side], want_send.at[side], want_recv.at[1 - side]
        )
        for side in range(2)
    ]
    for copy in want_copies:
        copy.start()
    sub = lax.broadcasted_iota(i32, (32, 128), 0)
    lane = lax.broadcasted_iota(i32, (32, 128), 1)
    x, yh = sub >> 1, sub & 1
    for face in range(6):
        axis, side = face // 2, face % 2
        if axis == 0:
            pick_index[face] = lane8
        elif axis == 1:
            pick_index[face] = 112 * side + (lane8 & 15)
        else:
            pick_index[face] = (lane8 & 7) * 16 + 15 * side
        for half in range(2):
            if axis == 0:
                mask = sub == 30 * side + half
            else:
                mask = ((x >> 3) == half) & ((lane >> 4) == (x & 7))
                if axis == 1:
                    mask = mask & (yh == side)
                else:
                    mask = mask & (((lane >> 3) & 1) == yh)
            pick_mask[face, half] = jnp.where(mask, 1.0, 0.0)
    spread_index[0] = lane
    spread_index[1] = (x & 7) * 16 + (lane & 15)
    spread_index[2] = (x & 7) * 16 + 8 * yh + (lane >> 4)
    grow_index[0] = (4 * yh + (lane >> 5)) * 16 + ((lane & 15) >> 1)
    grow_index[1] = (x >> 1) * 16 + ((lane & 15) >> 1)
    grow_index[2] = (x >> 1) * 16 + 4 * yh + (lane >> 5)

    loop(peers * CAP, invert, 8)

    for copy in want_copies:
        copy.wait()
    to_scalars = pltpu.make_async_copy(wants_in, wants_at, local_sem.at[1])
    to_scalars.start()
    to_scalars.wait()
    for peer in range(peers):
        code_rows[pl.ds(peer, 1), :] = codes_in[peer]
    for copy in block_copies:
        copy.wait()
    for side in range(2):
        for j in range(2):
            pool[SLOTS + 2 * side + j] = moved[side, j]

    def wait_payload(step):
        payload_copy(step + 1).wait_recv()

    for step in range(peers - 1):
        wait_payload(step)
    for place in range(CAP):
        payload_in[me * CAP + place] = answer(me, place)

    lane5 = lane_of(5)
    grow5 = [(4 * half + (lane5 >> 5)) * 16 + ((lane5 & 15) >> 1) for half in range(2)]
    for block in range(NEWB):
        for piece in range(OCTP):
            value = payload_in[request_slot[FACEREQ + block * OCTP + piece]]
            for part in range(2):
                for half in range(2):
                    grown = pick(value, grow5[half] + 8 * part)
                    for twin in range(2):
                        k = 2 * (4 * piece + 2 * part + twin) + half
                        made_rows[pl.ds(block * 160 + k, 5, stride=32), :] = grown

    for block in range(NEWB):
        for c in range(5):
            pool[10 + block, c] = made_rows[rows_of(block, c), :]

    def regrid(block):
        state_a[block] = pool[new_source[block]]

    loop(SLOTS, regrid, 2)

    def take_face(state, face_id, put):
        block, face = lax.div(face_id, 6), lax.rem(face_id, 6)
        index = pick_index[face]
        masks = [pick_mask[face, half].reshape(4, 8, 128) for half in range(2)]
        for c in range(5):
            value = state[block, c].reshape(4, 8, 128)
            picked = [pick(value[v], index) for v in range(4)]
            for half in range(2):
                rows = picked[0] * masks[half][0]
                for v in range(1, 4):
                    rows = rows + picked[v] * masks[half][v]
                put(c, half, jnp.sum(rows, axis=0, keepdims=True))

    def send_faces(step, state):
        def one(i):
            side, j = (i // 3, i % 3) if isinstance(i, int) else (lax.div(i, 3), lax.rem(i, 3))

            def put(c, half, row):
                faces_out[step][side, j, pl.ds(2 * c + half, 1), :] = row

            take_face(state, wants_at[side, 0, j], put)

        loop(6, one, 6)
        copies = [
            beside_copy(
                side,
                faces_out[step].at[side],
                faces_in[step].at[1 - side],
                face_send.at[step, side],
                face_recv.at[step, 1 - side],
            )
            for side in range(2)
        ]
        for copy in copies:
            copy.start()
        return copies

    def take_edges(state):
        def one(r):
            def put(c, half, row):
                edge_own[c, pl.ds(2 * r + half, 1), :] = row

            take_face(state, face_at[r], put)

        loop(FACEREQ, one, 6)

    def place_faces(step, state):
        def one(i):
            side, j = (i // 3, i % 3) if isinstance(i, int) else (lax.div(i, 3), lax.rem(i, 3))
            face = lax.rem(wants_out_face(side, j), 6)
            axis = lax.div(face, 2)
            index = spread_index[axis].reshape(4, 8, 128)
            odd = (lax.broadcasted_iota(i32, (8, 128), 0) & 1) == 1
            for c in range(5):
                first = jnp.broadcast_to(faces_in[step][side, j, pl.ds(2 * c, 1), :], (8, 128))
                second = jnp.broadcast_to(faces_in[step][side, j, pl.ds(2 * c + 1, 1), :], (8, 128))
                both_rows = jnp.where(odd, second, first)
                parts = []
                for v in range(4):
                    rows = jnp.where(axis == 0, both_rows, first if v < 2 else second)
                    parts.append(pick(rows, index[v]))
                state[SLOTS + i, c] = jnp.concatenate(parts, axis=0)

        loop(6, one, 6)

    def wants_out_face(side, j):
        return face_want[side * 3 + j]

    for j in range(6):
        face_want[j] = wants[j]

    def register_step(step):
        axis_row = jnp.zeros((16, 128), i32)
        sign_row = jnp.zeros((16, 128), f32)
        row = lax.broadcasted_iota(i32, (16, 128), 0) >> 1
        for r in range(FACEREQ):
            face = lax.rem(face_at[r], 6)
            axis_row = jnp.where(row == r, lax.div(face, 2), axis_row)
            sign_row = jnp.where(row == r, (2 * lax.rem(face, 2) - 1).astype(f32), sign_row)
        is_axis = [axis_row == axis for axis in range(3)]
        own = [edge_own[c] for c in range(5)]
        old = [edge_coarse[0, c] for c in range(5)]
        ghost = old
        if step == 1:
            ghost = [old[c] + 0.5 * (edge_coarse[1, c] - old[c]) for c in range(5)]

        def parts(state):
            inverse = 1.0 / state[0]
            normal = jnp.where(is_axis[0], state[1], jnp.where(is_axis[1], state[2], state[3]))
            kinetic = (state[1] * state[1] + state[2] * state[2] + state[3] * state[3]) * inverse
            pressure = 0.4 * state[4] - 0.2 * kinetic
            velocity = normal * inverse
            flux = [part * velocity for part in state]
            for axis in range(3):
                flux[1 + axis] = flux[1 + axis] + jnp.where(is_axis[axis], pressure, 0.0)
            flux[4] = flux[4] + pressure * velocity
            return flux, jnp.abs(velocity) + jnp.sqrt(1.4 * pressure * inverse)

        own_flux, own_speed = parts(own)
        ghost_flux, ghost_speed = parts(ghost)
        speed = jnp.maximum(own_speed, ghost_speed) * sign_row
        for c in range(5):
            value = 0.5 * (own_flux[c] + ghost_flux[c]) - 0.5 * speed * (ghost[c] - own[c])
            at = pl.ds(16 * c, 16)
            register[at, :] = value if step == 0 else register[at, :] + value

    copies = send_faces(0, state_a)
    edge_own[...] = jnp.ones((5, 16, 128), f32)
    edge_coarse[...] = jnp.ones((2, 5, 16, 128), f32)
    take_edges(state_a)

    def coarse_ghosts(r):
        slot = request_slot[r]
        axis = lax.div(lax.rem(face_at[r], 6), 2)
        index = grow_index[axis].reshape(4, 8, 128)
        value = payload_in[slot]
        for when in range(2):
            for half in range(2):
                grown = pick(value, grow5[half] + 8 * when)
                for c in range(5):
                    edge_coarse[when, c, pl.ds(2 * r + half, 1), :] = grown[c : c + 1]
        for c in range(5):
            rows = jnp.broadcast_to(value[c : c + 1], (8, 128))
            old = jnp.concatenate([pick(rows, index[v]) for v in range(4)], axis=0)
            new = jnp.concatenate([pick(rows, index[v] + 8) for v in range(4)], axis=0)
            state_a[SLOTS + 6 + r, c] = old
            state_b[SLOTS + 6 + r, c] = old + 0.5 * (new - old)

    loop(FACEREQ, coarse_ghosts, 2)
    register_step(0)
    for step in range(1, peers):
        payload_copy(step).wait_send()
    for copy in copies:
        copy.wait()
    place_faces(0, state_a)

    def first_step(block):
        def put(block, c, value):
            state_b[block, c] = value

        advance_block(state_a, put, block, ghost_index)

    loop(SLOTS, first_step)

    copies = send_faces(1, state_b)
    take_edges(state_b)
    register_step(1)

    lane16 = lane_of(16)
    shrink = ((lane16 >> 4) & 3) * 32 + 2 * (lane16 & 7)
    for c in range(5):
        value = register[16 * c : 16 * c + 16, :]
        value = value + pltpu.roll(value, 127, 1)
        value = value + pltpu.roll(value, 112, 1)
        value = value * 0.125
        register[16 * c : 16 * c + 16, :] = jnp.concatenate(
            [pick(value[:8], shrink[:8]), pick(value[8:], shrink[8:])], axis=0
        )
    for r in range(FACEREQ):
        first = register[pl.ds(2 * r, 5, stride=16), :]
        second = register[pl.ds(2 * r + 1, 5, stride=16), :]
        average[r] = jnp.where(lane5 < 64, first, second)

    def parcel_copy(step):
        index, device = peer_at(step)
        return pltpu.make_async_remote_copy(
            src_ref=parcel_out.at[pl.ds(step * 2, 2)],
            dst_ref=parcel_in.at[pl.ds(me * 2, 2)],
            send_sem=parcel_send.at[step],
            recv_sem=parcel_recv.at[step],
            device_id=device,
            device_id_type=MESH,
        )

    def parcel(row):
        first = average[slot_from[2 * row]]
        second = average[slot_from[2 * row + 1]]
        return jnp.where((lane5 & 15) < 8, first, second)

    for first in range(1, peers, 8):
        group = range(first, min(first + 8, peers))
        for step in group:
            index, _ = peer_at(step)
            for pair in range(2):
                parcel_out[step * 2 + pair] = parcel(index * 2 + pair)
        for step in group:
            parcel_copy(step).start()

    for copy in copies:
        copy.wait()
    place_faces(1, state_b)

    def second_step(block):
        def put(block, c, value):
            state_c[rows_of(block, c), :] = value

        advance_block(state_b, put, block, ghost_index)

    loop(SLOTS, second_step)

    def fold(i):
        c, k = lax.div(i, 32), lax.rem(i, 32)
        value = state_c[pl.ds(i, SLOTS, stride=160), :]
        fine_out[c, :, pl.ds(pl.multiple_of(k * 128, 128), 128)] = value

    loop(160, fold, 16)
    stores = [pltpu.make_async_copy(fine_out, fine_hand, store_sem.at[5])]
    stores[0].start()

    target = lax.broadcasted_iota(i32, (peers, 128), 1)
    wanted = jnp.where(target < 24 * CSLOTS, (target & 3) * 24 + (target >> 2), -7)
    chosen = []
    for half in range(2):
        picks = [
            (jnp.broadcast_to(code_rows[:, 2 * pair + half : 2 * pair + half + 1], (peers, 128)) == wanted)
            for pair in range(2)
        ]
        chosen.append(
            jnp.concatenate([jnp.where(p, 1.0, 0.0) for p in picks], axis=0).astype(jnp.bfloat16)
        )

    def contract(left, right):
        return lax.dot_general(
            left, right, (((0,), (0,)), ((), ())), preferred_element_type=f32
        )

    ones = jnp.ones((2 * peers, 128), jnp.bfloat16)
    counts = contract(chosen[0], ones) + contract(chosen[1], ones)
    loads[3].wait()

    def wait_parcel(step):
        parcel_copy(step + 1).wait()

    for step in range(peers - 1):
        wait_parcel(step)
    for pair in range(2):
        parcel_in[me * 2 + pair] = parcel(me * 2 + pair)

    def line_up(peer):
        for pair in range(2):
            gathered[pl.ds(pair * peers + peer, 5, stride=2 * peers), :] = parcel_in[peer * 2 + pair]

    loop(peers, line_up, 8)
    low8, low4 = (lane8 & 15) < 8, (lane4 & 15) < 8
    for c in range(5):
        value = gathered[pl.ds(c * 2 * peers, 2 * peers), :]
        coarse_part = value.astype(jnp.bfloat16)
        rest = (value - coarse_part.astype(f32)).astype(jnp.bfloat16)
        sums = [contract(chosen[h], coarse_part) + contract(chosen[h], rest) for h in range(2)]
        change = {}
        for face in range(6):
            scale = 0.08 if face % 2 else -0.08
            for half in range(2):
                at = (face * 2 + half) * 8
                first, second = sums[0][at : at + 8], sums[1][at : at + 8]
                count = counts[at : at + 8]
                lows = first + pltpu.roll(second, 120, 1)
                highs = second + pltpu.roll(first, 8, 1)
                total = jnp.where(low4, lows[:4], highs[4:])
                number = jnp.where(low4, count[:4], count[4:])
                flux = flux_in[face, c, :, pl.ds(half * 128, 128)]
                change[face, half] = scale * (number * flux - total)
        stacked = {
            face: jnp.concatenate([change[face, 0], change[face, 1]], axis=0) for face in range(2, 6)
        }
        for x8 in range(8):
            for yh8 in range(2):
                shift = (112 * yh8 - 16 * x8) % 128
                moved = stacked[2 + yh8]
                moved = moved if shift == 0 else pltpu.roll(moved, shift, 1)
                added = jnp.where((lane8 >> 4) == 7 * yh8, moved, 0.0)
                index = x8 * 16 + 8 * yh8 + (lane8 >> 4)
                added = added + jnp.where((lane8 & 15) == 0, pick(stacked[4], index), 0.0)
                added = added + jnp.where((lane8 & 15) == 15, pick(stacked[5], index), 0.0)
                for upper in range(2):
                    x_at = 8 * upper + x8
                    at = pl.ds((2 * x_at + yh8) * 128, 128)
                    value = new_in[c, :, at] + added[4 * upper : 4 * upper + 4]
                    if x_at == 0:
                        value = value + change[0, yh8]
                    if x_at == 15:
                        value = value + change[1, yh8]
                    coarse_out[c, :, at] = value
        store = pltpu.make_async_copy(coarse_out.at[c], coarse_hand.at[c], store_sem.at[c])
        store.start()
        stores.append(store)
    for store in stores:
        store.wait()


def hand_over(fine, coarse, fine_out, coarse_out, fine_stage, coarse_stage, in_sem, out_sem):
    trips = []
    for c in range(5):
        for k, (source, stage, target) in enumerate(
            ((fine, fine_stage, fine_out), (coarse, coarse_stage, coarse_out))
        ):
            trips.append(
                (
                    pltpu.make_async_copy(source.at[c], stage.at[c], in_sem.at[2 * c + k]),
                    pltpu.make_async_copy(stage.at[c], target.at[c], out_sem.at[2 * c + k]),
                )
            )
    for arrive, _ in trips:
        arrive.start()
    for arrive, leave in trips:
        arrive.wait()
        leave.start()
    for _, leave in trips:
        leave.wait()


def on_device(sizes, fine_old, send_left, send_right, new_source, face_source, request_slot, request_code,
              coarse_old, coarse_new, coarse_flux):
    peers = sizes[1] * sizes[2]
    smem = pl.BlockSpec(memory_space=pltpu.SMEM)
    hbm = pl.BlockSpec(memory_space=pltpu.HBM)
    dma = pltpu.SemaphoreType.DMA
    V = pltpu.VMEM
    fine, coarse = pl.pallas_call(
        functools.partial(kernel, sizes),
        out_shape=(
            jax.ShapeDtypeStruct((5, SLOTS, 4096), f32),
            jax.ShapeDtypeStruct((5, CSLOTS, 4096), f32),
        ),
        in_specs=[smem] * 6 + [hbm] * 4,
        out_specs=(hbm, hbm),
        scratch_shapes=[
            V((5, SLOTS, 4096), f32),
            V((5, CSLOTS, 4096), f32),
            V((5, CSLOTS, 4096), f32),
            V((6, 5, CSLOTS, 256), f32),
            V((peers, 1, 128), i32),
            V((peers, 1, 128), i32),
            pltpu.SMEM((peers, 1, 128), i32),
            V((2, 1, 128), i32),
            V((2, 1, 128), i32),
            pltpu.SMEM((2, 1, 128), i32),
            pltpu.SMEM((FACES,), i32),
            pltpu.SMEM((8,), i32),
            pltpu.SMEM((peers * CAP,), i32),
            pltpu.SMEM((8,), i32),
            V((8 * 160, 128), f32),
            V((416, 128), f32),
            V((2816, 128), f32),
            V((SLOTS, 5, 32, 128), f32),
            V((12, 5, 32, 128), f32),
            V((2, 2, 5, 32, 128), f32),
            V((2, 2, 5, 32, 128), f32),
            V((224, 8, 128), f32),
            V((peers * CAP, 5, 128), f32),
            V((peers * CAP, 5, 128), f32),
            V((18, 5, 32, 128), f32),
            V((18, 5, 32, 128), f32),
            V((8 * 160, 128), f32),
            V((6, 8, 128), i32),
            V((6, 2, 32, 128), f32),
            V((3, 32, 128), i32),
            V((3, 32, 128), i32),
            V((2, 3, 10, 128), f32),
            V((2, 3, 10, 128), f32),
            V((2, 3, 10, 128), f32),
            V((2, 3, 10, 128), f32),
            V((5, 16, 128), f32),
            V((2, 5, 16, 128), f32),
            V((128, 128), f32),
            V((FACEREQ, 5, 128), f32),
            V((peers * 2, 5, 128), f32),
            V((peers * 2, 5, 128), f32),
            V((8 * 2 * peers, 128), f32),
            V((peers, 128), i32),
            V((5, SLOTS, 4096), f32),
            V((5, CSLOTS, 4096), f32),
            dma((6,)),
            dma((4,)),
            dma((2,)),
            dma((peers,)),
            dma((peers,)),
            dma((2,)),
            dma((2,)),
            dma((2,)),
            dma((2,)),
            dma((peers,)),
            dma((peers,)),
            dma((2, 2)),
            dma((2, 2)),
            dma((peers,)),
            dma((peers,)),
        ],
        compiler_params=pltpu.CompilerParams(
            collective_id=0, has_side_effects=True, vmem_limit_bytes=64 * 1024 * 1024
        ),
    )(
        send_left,
        send_right,
        new_source,
        face_source,
        request_slot,
        request_code,
        jnp.transpose(fine_old, (1, 0, 2)),
        jnp.transpose(coarse_old, (1, 0, 2)),
        jnp.transpose(coarse_new, (1, 0, 2)),
        jnp.transpose(coarse_flux, (1, 2, 0, 3)),
    )
    fine, coarse = pl.pallas_call(
        hand_over,
        out_shape=(
            jax.ShapeDtypeStruct((5, SLOTS, 4096), f32),
            jax.ShapeDtypeStruct((5, CSLOTS, 4096), f32),
        ),
        in_specs=[hbm, hbm],
        out_specs=(hbm, hbm),
        scratch_shapes=[
            V((5, SLOTS, 4096), f32),
            V((5, CSLOTS, 4096), f32),
            dma((10,)),
            dma((10,)),
        ],
        compiler_params=pltpu.CompilerParams(vmem_limit_bytes=64 * 1024 * 1024),
    )(fine, coarse)
    return jnp.transpose(fine, (1, 0, 2)), jnp.transpose(coarse, (1, 0, 2))


def solution(mesh):
    sizes = (mesh.shape["gx"], mesh.shape["gy"], mesh.shape["gz"])
    every = ("gx", "gy", "gz")
    in_specs = (
        P(every, None, None),
        P(every),
        P(every),
        P(every),
        P(every, None),
        P(every),
        P(every),
        P(every, None, None),
        P(every, None, None),
        P(every, None, None, None),
    )
    out_specs = (P(every, None, None), P(every, None, None))
    return jax.shard_map(
        functools.partial(on_device, sizes), mesh=mesh, in_specs=in_specs, out_specs=out_specs, check_vma=False
    )
```

```python
import functools

import jax
import jax.numpy as jnp
from jax import lax
from jax.experimental import pallas as pl
from jax.experimental.pallas import tpu as pltpu
from jax.sharding import PartitionSpec as P

MESH = pl.DeviceIdType.MESH
SLOTS = 6
CSLOTS = 4
CAP = 4
FACES = 36
FACEREQ = 6
REQ = 14
NEWB = 2
OCTP = 4
f32 = jnp.float32
i32 = jnp.int32


def pick(x, idx):
    return jnp.take_along_axis(x, idx, axis=1, mode="promise_in_bounds")


def loop(count, body, unroll=1):
    def step(i, carry):
        for part in range(unroll):
            body(i * unroll + part)
        return carry

    lax.fori_loop(0, count // unroll, step, 0)
    for i in range(count - count % unroll, count):
        body(i)


def lane_of(rows):
    return lax.broadcasted_iota(i32, (rows, 128), 1)


def merge_halves(first, second, rows):
    low = (lane_of(rows) & 15) < 8
    return (
        jnp.where(low, first, pltpu.roll(second, 8, 1)),
        jnp.where(low, pltpu.roll(first, 120, 1), second),
    )


def flux_and_speed(state, axis):
    density, energy = state[0], state[4]
    inverse = 1.0 / density
    kinetic = (state[1] * state[1] + state[2] * state[2] + state[3] * state[3]) * inverse
    pressure = 0.4 * energy - 0.2 * kinetic
    velocity = state[1 + axis] * inverse
    flux = [part * velocity for part in state]
    flux[1 + axis] = flux[1 + axis] + pressure
    flux[4] = flux[4] + pressure * velocity
    return flux, jnp.abs(velocity) + jnp.sqrt(1.4 * pressure * inverse)


def shifted_x(own, ghost_low, ghost_high):
    sub = lax.broadcasted_iota(i32, (4, 8, 128), 1)
    down = pltpu.roll(own, 2, 1)
    entering = pltpu.roll(ghost_low[3], 2, 0)
    low = jnp.where(sub < 2, jnp.concatenate([entering[None], down[:3]], axis=0), down)
    up = pltpu.roll(own, 6, 1)
    entering = pltpu.roll(ghost_high[0], 6, 0)
    high = jnp.where(sub >= 6, jnp.concatenate([up[1:], entering[None]], axis=0), up)
    return low, high


def swap_rows(value, odd):
    return jnp.where(odd, pltpu.roll(value, 1, 1), pltpu.roll(value, 7, 1))


def shifted_y(own, ghost_low, ghost_high):
    odd = (lax.broadcasted_iota(i32, (4, 8, 128), 1) & 1) == 1
    lane = lax.broadcasted_iota(i32, (4, 8, 128), 2)
    low = swap_rows(jnp.where(odd, ghost_low, own), odd)
    low = pltpu.roll(jnp.where(lane >= 112, low, own), 16, 2)
    high = swap_rows(jnp.where(odd, own, ghost_high), odd)
    high = pltpu.roll(jnp.where(lane < 16, high, own), 112, 2)
    return low, high


def shifted_z(own, ghost_low, ghost_high):
    z = lax.broadcasted_iota(i32, (4, 8, 128), 2) & 15
    low = jnp.where(z == 0, pltpu.roll(ghost_low, 113, 2), pltpu.roll(own, 1, 2))
    high = jnp.where(z == 15, pltpu.roll(ghost_high, 15, 2), pltpu.roll(own, 127, 2))
    return low, high


def advance_block(source, put, block, ghost_index):
    shape = (4, 8, 128)
    own = [source[block, c].reshape(shape) for c in range(5)]
    inverse = 1.0 / own[0]
    kinetic = (own[1] * own[1] + own[2] * own[2] + own[3] * own[3]) * inverse
    pressure = 0.4 * own[4] - 0.2 * kinetic
    sound = jnp.sqrt(1.4 * pressure * inverse)
    total = [None] * 5
    for axis, shifted in enumerate((shifted_x, shifted_y, shifted_z)):
        low_at = ghost_index[block * 6 + 2 * axis]
        high_at = ghost_index[block * 6 + 2 * axis + 1]
        low, high = [], []
        for c in range(5):
            below, above = shifted(
                own[c], source[low_at, c].reshape(shape), source[high_at, c].reshape(shape)
            )
            low.append(below)
            high.append(above)
        speed = jnp.abs(own[1 + axis] * inverse) + sound
        low_flux, low_speed = flux_and_speed(low, axis)
        high_flux, high_speed = flux_and_speed(high, axis)
        low_speed = jnp.maximum(low_speed, speed)
        high_speed = jnp.maximum(high_speed, speed)
        for c in range(5):
            part = high_flux[c] - low_flux[c]
            part = part + low_speed * (own[c] - low[c]) - high_speed * (high[c] - own[c])
            total[c] = part if axis == 0 else total[c] + part
    for c in range(5):
        put(block, c, (own[c] - 0.04 * total[c]).reshape(32, 128))


def kernel(
    sizes,
    send_left,
    send_right,
    new_source,
    face_source,
    request_slot,
    request_code,
    fine_hbm,
    old_hbm,
    new_hbm,
    flux_hbm,
    fine_hand,
    coarse_hand,
    fine_in,
    old_in,
    new_in,
    flux_in,
    codes_out,
    codes_in,
    codes_at,
    wants_out,
    wants_in,
    wants_at,
    ghost_index,
    face_at,
    slot_from,
    face_want,
    own_rows,
    made_rows,
    table_rows,
    own_flat,
    pool,
    moved,
    bundle,
    table,
    payload_out,
    payload_in,
    state_a,
    state_b,
    state_c,
    pick_index,
    pick_mask,
    spread_index,
    grow_index,
    faces_out_a,
    faces_out_b,
    faces_in_a,
    faces_in_b,
    edge_own,
    edge_coarse,
    register,
    average,
    parcel_out,
    parcel_in,
    gathered,
    code_rows,
    fine_out,
    coarse_out,
    store_sem,
    load_sem,
    local_sem,
    code_send,
    code_recv,
    want_send,
    want_recv,
    block_send,
    block_recv,
    payload_send,
    payload_recv,
    face_send,
    face_recv,
    parcel_send,
    parcel_recv,
):
    n_gx, n_gy, n_gz = sizes
    peers = n_gy * n_gz
    ranks = n_gx * peers
    gx, gy, gz = lax.axis_index("gx"), lax.axis_index("gy"), lax.axis_index("gz")
    me = gy * n_gz + gz
    rank = gx * peers + me

    at_y = [gy] + [lax.rem(gy + step, n_gy) for step in range(1, n_gy)]
    at_z = [gz] + [lax.rem(gz + step, n_gz) for step in range(1, n_gz)]

    def peer_at(step):
        y, z = at_y[step // n_gz], at_z[step % n_gz]
        return y * n_gz + z, (gx, y, z)

    def on_curve(index):
        return (lax.div(index, peers), lax.rem(lax.div(index, n_gz), n_gy), lax.rem(index, n_gz))

    beside = (on_curve(lax.rem(rank + ranks - 1, ranks)), on_curve(lax.rem(rank + 1, ranks)))

    faces_out, faces_in = (faces_out_a, faces_out_b), (faces_in_a, faces_in_b)
    barrier = pltpu.get_barrier_semaphore()

    def greet(step):
        pl.semaphore_signal(barrier, inc=1, device_id=peer_at(step + 1)[1], device_id_type=MESH)

    for step in range(peers - 1):
        greet(step)
    for device in beside:
        pl.semaphore_signal(barrier, inc=1, device_id=device, device_id_type=MESH)

    loads = [
        pltpu.make_async_copy(fine_hbm, fine_in, load_sem.at[0]),
        pltpu.make_async_copy(old_hbm, old_in, load_sem.at[1]),
        pltpu.make_async_copy(new_hbm, new_in, load_sem.at[2]),
        pltpu.make_async_copy(flux_hbm, flux_in, load_sem.at[3]),
    ]
    for load in loads:
        load.start()

    lane1 = lane_of(1)
    place_of = lax.broadcasted_iota(i32, (peers, 128), 0) * CAP + lane_of(peers)
    rows = jnp.full((peers, 128), -1, i32)
    for r in range(REQ):
        rows = jnp.where(place_of == request_slot[r], request_code[r], rows)
    code_rows[...] = jnp.where(lane_of(peers) < CAP, rows, -1)
    for peer in range(peers):
        codes_out[peer] = code_rows[pl.ds(peer, 1), :]

    def rows_of(block, c):
        return pl.ds(pl.multiple_of((block * 5 + c) * 32, 32), 32)

    loads[0].wait()

    def unfold(i):
        c, k = lax.div(i, 32), lax.rem(i, 32)
        value = fine_in[c, :, pl.ds(pl.multiple_of(k * 128, 128), 128)]
        own_rows[pl.ds(i, SLOTS, stride=160), :] = value

    loop(160, unfold, 16)

    def split_own(block):
        for c in range(5):
            value = own_rows[rows_of(block, c), :]
            own_flat[block, c] = value
            pool[block, c] = value

    loop(SLOTS, split_own, 2)
    for side, listed in enumerate((send_left, send_right)):
        for j in range(2):
            bundle[side, j] = own_flat[listed[j]]

    loads[1].wait()
    loads[2].wait()
    lane8, lane4 = lane_of(8), lane_of(4)

    def both(c, k):
        at = pl.ds(k * 128, 128)
        return old_in[c, :, at], new_in[c, :, at]

    def put_face(c, face, quadrant, value):
        table_rows[pl.ds((face * 4 + quadrant) * 8 + c, CSLOTS, stride=24 * 8), :] = value

    def fill_table(c):
        for side in range(2):
            for half in range(2):
                first, second = both(c, 30 * side + half)
                for low, value in enumerate(merge_halves(first, second, 4)):
                    put_face(c, side, half * 2 + low, value)
        for side in range(2):

            def fill_y(half, side=side):
                rows = jnp.zeros((8, 128), f32)
                for x in range(8):
                    value = jnp.concatenate(both(c, half * 16 + 2 * x + side), axis=0)
                    shift = (16 * x - 112 * side) % 128
                    value = value if shift == 0 else pltpu.roll(value, shift, 1)
                    rows = jnp.where((lane8 >> 4) == x, value, rows)
                for low, value in enumerate(merge_halves(rows[:4], rows[4:], 4)):
                    put_face(c, 2 + side, half * 2 + low, value)

            for half in range(2):
                fill_y(half)

            def fill_z(quadrant, side=side):
                rows = jnp.zeros((8, 128), f32)
                index = (lane8 & 7) * 16 + 15 * side
                for x in range(8):
                    k = (quadrant // 2) * 16 + 2 * x + quadrant % 2
                    value = pick(jnp.concatenate(both(c, k), axis=0), index)
                    rows = jnp.where((lane8 >> 4) == x, value, rows)
                put_face(c, 4 + side, quadrant, jnp.where((lane4 & 15) < 8, rows[:4], rows[4:]))

            for quadrant in range(4):
                fill_z(quadrant)

        def fill_octant(i):
            half, pair = i // 8, i % 8
            at = (4 * pair + half) * 128
            first = old_in[c, :, pl.ds(at, 128)]
            second = old_in[c, :, pl.ds(at + 256, 128)]
            for low, value in enumerate(merge_halves(first, second, 4)):
                code = 96 + ((pair // 4) * 4 + half * 2 + low) * 4 + pair % 4
                table_rows[pl.ds(code * 8 + c, CSLOTS, stride=32 * 8), :] = value

        for i in range(16):
            fill_octant(i)

    loop(5, fill_table)

    def split_table(code):
        table[code] = table_rows[pl.ds(pl.multiple_of(code * 8, 8), 8), :]

    loop(224, split_table, 16)
    def scan(i, carry):
        count, wants, places = carry
        e = face_source[lax.div(i, 6), lax.rem(i, 6)]
        is_left = e < FACES
        is_right = (e >= 2 * FACES) & (e < 3 * FACES)
        index = jnp.where(
            is_left,
            SLOTS + jnp.minimum(count[0], 2),
            jnp.where(
                is_right,
                SLOTS + 3 + jnp.minimum(count[1], 2),
                jnp.where(e >= 3 * FACES, SLOTS + 6 + e - 3 * FACES, lax.div(jnp.maximum(e - FACES, 0), 6)),
            ),
        )
        ghost_index[i] = index
        new_wants = tuple(
            jnp.where(is_left & (count[0] == j), e, wants[j]) for j in range(3)
        ) + tuple(
            jnp.where(is_right & (count[1] == j), e - 2 * FACES, wants[3 + j]) for j in range(3)
        )
        new_places = tuple(
            jnp.where(e == 3 * FACES + r, i, places[r]) for r in range(FACEREQ)
        )
        new_count = (
            count[0] + jnp.where(is_left, 1, 0),
            count[1] + jnp.where(is_right, 1, 0),
        )
        return new_count, new_wants, new_places

    zero = jnp.int32(0)
    _, wants, places = lax.fori_loop(
        0, FACES, scan, ((zero, zero), (zero,) * 6, (zero,) * FACEREQ)
    )
    for r in range(FACEREQ):
        face_at[r] = places[r]
    for side in range(2):
        row = jnp.zeros((1, 128), i32)
        for j in range(3):
            row = jnp.where(lane1 == j, wants[3 * side + j], row)
        wants_out[side] = row

    def invert(slot):
        found = jnp.int32(0)
        for r in range(FACEREQ):
            found = jnp.where(request_slot[r] == slot, r, found)
        slot_from[slot] = found

    sub = lax.broadcasted_iota(i32, (32, 128), 0)
    lane = lax.broadcasted_iota(i32, (32, 128), 1)
    x, yh = sub >> 1, sub & 1
    for face in range(6):
        axis, side = face // 2, face % 2
        if axis == 0:
            pick_index[face] = lane8
        elif axis == 1:
            pick_index[face] = 112 * side + (lane8 & 15)
        else:
            pick_index[face] = (lane8 & 7) * 16 + 15 * side
        for half in range(2):
            if axis == 0:
                mask = sub == 30 * side + half
            else:
                mask = ((x >> 3) == half) & ((lane >> 4) == (x & 7))
                if axis == 1:
                    mask = mask & (yh == side)
                else:
                    mask = mask & (((lane >> 3) & 1) == yh)
            pick_mask[face, half] = jnp.where(mask, 1.0, 0.0)
    spread_index[0] = lane
    spread_index[1] = (x & 7) * 16 + (lane & 15)
    spread_index[2] = (x & 7) * 16 + 8 * yh + (lane >> 4)
    grow_index[0] = (4 * yh + (lane >> 5)) * 16 + ((lane & 15) >> 1)
    grow_index[1] = (x >> 1) * 16 + ((lane & 15) >> 1)
    grow_index[2] = (x >> 1) * 16 + 4 * yh + (lane >> 5)

    loop(peers * CAP, invert, 8)
    pl.semaphore_wait(barrier, peers + 1)

    def code_copy(step):
        index, device = peer_at(step)
        return pltpu.make_async_remote_copy(
            src_ref=codes_out.at[index],
            dst_ref=codes_in.at[me],
            send_sem=code_send.at[step],
            recv_sem=code_recv.at[step],
            device_id=device,
            device_id_type=MESH,
        )

    def start_codes(step):
        code_copy(step + 1).start()

    for step in range(peers - 1):
        start_codes(step)

    def beside_copy(side, source, target, send, recv):
        return pltpu.make_async_remote_copy(
            src_ref=source,
            dst_ref=target,
            send_sem=send,
            recv_sem=recv,
            device_id=beside[side],
            device_id_type=MESH,
        )

    want_copies = [
        beside_copy(
            side, wants_out.at[side], wants_in.at[1 - side], want_send.at[side], want_recv.at[1 - side]
        )
        for side in range(2)
    ]
    for copy in want_copies:
        copy.start()
    block_copies = [
        beside_copy(
            side,
            bundle.at[side],
            moved.at[1 - side],
            block_send.at[side],
            block_recv.at[1 - side],
        )
        for side in range(2)
    ]
    for copy in block_copies:
        copy.start()


    def wait_codes(step):
        code_copy(step + 1).wait_recv()

    for step in range(peers - 1):
        wait_codes(step)
    codes_in[me] = codes_out[me]
    to_scalars = pltpu.make_async_copy(codes_in, codes_at, local_sem.at[0])
    to_scalars.start()
    to_scalars.wait()

    def answer(peer, place):
        code = jnp.maximum(codes_at[peer, 0, place], 0)
        return table[code][:5]

    def payload_copy(step):
        index, device = peer_at(step)
        return pltpu.make_async_remote_copy(
            src_ref=payload_out.at[pl.ds(step * CAP, CAP)],
            dst_ref=payload_in.at[pl.ds(me * CAP, CAP)],
            send_sem=payload_send.at[step],
            recv_sem=payload_recv.at[step],
            device_id=device,
            device_id_type=MESH,
        )

    for first in range(1, peers, 8):
        group = range(first, min(first + 8, peers))
        for step in group:
            index, _ = peer_at(step)
            for place in range(CAP):
                payload_out[step * CAP + place] = answer(index, place)
        for step in group:
            payload_copy(step).start()
    for step in range(1, peers):
        code_copy(step).wait_send()


    for copy in want_copies:
        copy.wait()
    to_scalars = pltpu.make_async_copy(wants_in, wants_at, local_sem.at[1])
    to_scalars.start()
    to_scalars.wait()
    for peer in range(peers):
        code_rows[pl.ds(peer, 1), :] = codes_in[peer]
    for copy in block_copies:
        copy.wait()
    for side in range(2):
        for j in range(2):
            pool[SLOTS + 2 * side + j] = moved[side, j]

    def wait_payload(step):
        payload_copy(step + 1).wait_recv()

    for step in range(peers - 1):
        wait_payload(step)
    for place in range(CAP):
        payload_in[me * CAP + place] = answer(me, place)

    lane5 = lane_of(5)
    grow5 = [(4 * half + (lane5 >> 5)) * 16 + ((lane5 & 15) >> 1) for half in range(2)]
    for block in range(NEWB):
        for piece in range(OCTP):
            value = payload_in[request_slot[FACEREQ + block * OCTP + piece]]
            for part in range(2):
                for half in range(2):
                    grown = pick(value, grow5[half] + 8 * part)
                    for twin in range(2):
                        k = 2 * (4 * piece + 2 * part + twin) + half
                        made_rows[pl.ds(block * 160 + k, 5, stride=32), :] = grown

    for block in range(NEWB):
        for c in range(5):
            pool[10 + block, c] = made_rows[rows_of(block, c), :]

    def regrid(block):
        state_a[block] = pool[new_source[block]]

    loop(SLOTS, regrid, 2)

    def take_face(state, face_id, put):
        block, face = lax.div(face_id, 6), lax.rem(face_id, 6)
        index = pick_index[face]
        masks = [pick_mask[face, half].reshape(4, 8, 128) for half in range(2)]
        for c in range(5):
            value = state[block, c].reshape(4, 8, 128)
            picked = [pick(value[v], index) for v in range(4)]
            for half in range(2):
                rows = picked[0] * masks[half][0]
                for v in range(1, 4):
                    rows = rows + picked[v] * masks[half][v]
                put(c, half, jnp.sum(rows, axis=0, keepdims=True))

    def send_faces(step, state):
        def one(i):
            side, j = (i // 3, i % 3) if isinstance(i, int) else (lax.div(i, 3), lax.rem(i, 3))

            def put(c, half, row):
                faces_out[step][side, j, pl.ds(2 * c + half, 1), :] = row

            take_face(state, wants_at[side, 0, j], put)

        loop(6, one, 6)
        copies = [
            beside_copy(
                side,
                faces_out[step].at[side],
                faces_in[step].at[1 - side],
                face_send.at[step, side],
                face_recv.at[step, 1 - side],
            )
            for side in range(2)
        ]
        for copy in copies:
            copy.start()
        return copies

    def take_edges(state):
        def one(r):
            def put(c, half, row):
                edge_own[c, pl.ds(2 * r + half, 1), :] = row

            take_face(state, face_at[r], put)

        loop(FACEREQ, one, 6)

    def place_faces(step, state):
        def one(i):
            side, j = (i // 3, i % 3) if isinstance(i, int) else (lax.div(i, 3), lax.rem(i, 3))
            face = lax.rem(wants_out_face(side, j), 6)
            axis = lax.div(face, 2)
            index = spread_index[axis].reshape(4, 8, 128)
            odd = (lax.broadcasted_iota(i32, (8, 128), 0) & 1) == 1
            for c in range(5):
                first = jnp.broadcast_to(faces_in[step][side, j, pl.ds(2 * c, 1), :], (8, 128))
                second = jnp.broadcast_to(faces_in[step][side, j, pl.ds(2 * c + 1, 1), :], (8, 128))
                both_rows = jnp.where(odd, second, first)
                parts = []
                for v in range(4):
                    rows = jnp.where(axis == 0, both_rows, first if v < 2 else second)
                    parts.append(pick(rows, index[v]))
                state[SLOTS + i, c] = jnp.concatenate(parts, axis=0)

        loop(6, one, 6)

    def wants_out_face(side, j):
        return face_want[side * 3 + j]

    for j in range(6):
        face_want[j] = wants[j]

    def register_step(step):
        axis_row = jnp.zeros((16, 128), i32)
        sign_row = jnp.zeros((16, 128), f32)
        row = lax.broadcasted_iota(i32, (16, 128), 0) >> 1
        for r in range(FACEREQ):
            face = lax.rem(face_at[r], 6)
            axis_row = jnp.where(row == r, lax.div(face, 2), axis_row)
            sign_row = jnp.where(row == r, (2 * lax.rem(face, 2) - 1).astype(f32), sign_row)
        is_axis = [axis_row == axis for axis in range(3)]
        own = [edge_own[c] for c in range(5)]
        old = [edge_coarse[0, c] for c in range(5)]
        ghost = old
        if step == 1:
            ghost = [old[c] + 0.5 * (edge_coarse[1, c] - old[c]) for c in range(5)]

        def parts(state):
            inverse = 1.0 / state[0]
            normal = jnp.where(is_axis[0], state[1], jnp.where(is_axis[1], state[2], state[3]))
            kinetic = (state[1] * state[1] + state[2] * state[2] + state[3] * state[3]) * inverse
            pressure = 0.4 * state[4] - 0.2 * kinetic
            velocity = normal * inverse
            flux = [part * velocity for part in state]
            for axis in range(3):
                flux[1 + axis] = flux[1 + axis] + jnp.where(is_axis[axis], pressure, 0.0)
            flux[4] = flux[4] + pressure * velocity
            return flux, jnp.abs(velocity) + jnp.sqrt(1.4 * pressure * inverse)

        own_flux, own_speed = parts(own)
        ghost_flux, ghost_speed = parts(ghost)
        speed = jnp.maximum(own_speed, ghost_speed) * sign_row
        for c in range(5):
            value = 0.5 * (own_flux[c] + ghost_flux[c]) - 0.5 * speed * (ghost[c] - own[c])
            at = pl.ds(16 * c, 16)
            register[at, :] = value if step == 0 else register[at, :] + value

    copies = send_faces(0, state_a)
    edge_own[...] = jnp.ones((5, 16, 128), f32)
    edge_coarse[...] = jnp.ones((2, 5, 16, 128), f32)
    take_edges(state_a)

    def coarse_ghosts(r):
        slot = request_slot[r]
        axis = lax.div(lax.rem(face_at[r], 6), 2)
        index = grow_index[axis].reshape(4, 8, 128)
        value = payload_in[slot]
        for when in range(2):
            for half in range(2):
                grown = pick(value, grow5[half] + 8 * when)
                for c in range(5):
                    edge_coarse[when, c, pl.ds(2 * r + half, 1), :] = grown[c : c + 1]
        for c in range(5):
            rows = jnp.broadcast_to(value[c : c + 1], (8, 128))
            old = jnp.concatenate([pick(rows, index[v]) for v in range(4)], axis=0)
            new = jnp.concatenate([pick(rows, index[v] + 8) for v in range(4)], axis=0)
            state_a[SLOTS + 6 + r, c] = old
            state_b[SLOTS + 6 + r, c] = old + 0.5 * (new - old)

    loop(FACEREQ, coarse_ghosts, 2)
    register_step(0)
    for step in range(1, peers):
        payload_copy(step).wait_send()
    for copy in copies:
        copy.wait()
    place_faces(0, state_a)

    def first_step(block):
        def put(block, c, value):
            state_b[block, c] = value

        advance_block(state_a, put, block, ghost_index)

    loop(SLOTS, first_step)

    copies = send_faces(1, state_b)
    take_edges(state_b)
    register_step(1)

    lane16 = lane_of(16)
    shrink = ((lane16 >> 4) & 3) * 32 + 2 * (lane16 & 7)
    for c in range(5):
        value = register[16 * c : 16 * c + 16, :]
        value = value + pltpu.roll(value, 127, 1)
        value = value + pltpu.roll(value, 112, 1)
        value = value * 0.125
        register[16 * c : 16 * c + 16, :] = jnp.concatenate(
            [pick(value[:8], shrink[:8]), pick(value[8:], shrink[8:])], axis=0
        )
    for r in range(FACEREQ):
        first = register[pl.ds(2 * r, 5, stride=16), :]
        second = register[pl.ds(2 * r + 1, 5, stride=16), :]
        average[r] = jnp.where(lane5 < 64, first, second)

    def parcel_copy(step):
        index, device = peer_at(step)
        return pltpu.make_async_remote_copy(
            src_ref=parcel_out.at[pl.ds(step * 2, 2)],
            dst_ref=parcel_in.at[pl.ds(me * 2, 2)],
            send_sem=parcel_send.at[step],
            recv_sem=parcel_recv.at[step],
            device_id=device,
            device_id_type=MESH,
        )

    def parcel(row):
        first = average[slot_from[2 * row]]
        second = average[slot_from[2 * row + 1]]
        return jnp.where((lane5 & 15) < 8, first, second)

    for first in range(1, peers, 8):
        group = range(first, min(first + 8, peers))
        for step in group:
            index, _ = peer_at(step)
            for pair in range(2):
                parcel_out[step * 2 + pair] = parcel(index * 2 + pair)
        for step in group:
            parcel_copy(step).start()

    for copy in copies:
        copy.wait()
    place_faces(1, state_b)

    def second_step(block):
        def put(block, c, value):
            state_c[rows_of(block, c), :] = value

        advance_block(state_b, put, block, ghost_index)

    loop(SLOTS, second_step)

    def fold(i):
        c, k = lax.div(i, 32), lax.rem(i, 32)
        value = state_c[pl.ds(i, SLOTS, stride=160), :]
        fine_out[c, :, pl.ds(pl.multiple_of(k * 128, 128), 128)] = value

    loop(160, fold, 16)
    stores = [pltpu.make_async_copy(fine_out, fine_hand, store_sem.at[5])]
    stores[0].start()

    target = lax.broadcasted_iota(i32, (peers, 128), 1)
    wanted = jnp.where(target < 24 * CSLOTS, (target & 3) * 24 + (target >> 2), -7)
    chosen = []
    for half in range(2):
        picks = [
            (jnp.broadcast_to(code_rows[:, 2 * pair + half : 2 * pair + half + 1], (peers, 128)) == wanted)
            for pair in range(2)
        ]
        chosen.append(
            jnp.concatenate([jnp.where(p, 1.0, 0.0) for p in picks], axis=0).astype(jnp.bfloat16)
        )

    def contract(left, right):
        return lax.dot_general(
            left, right, (((0,), (0,)), ((), ())), preferred_element_type=f32
        )

    ones = jnp.ones((2 * peers, 128), jnp.bfloat16)
    counts = contract(chosen[0], ones) + contract(chosen[1], ones)
    loads[3].wait()

    def wait_parcel(step):
        parcel_copy(step + 1).wait()

    for step in range(peers - 1):
        wait_parcel(step)
    for pair in range(2):
        parcel_in[me * 2 + pair] = parcel(me * 2 + pair)

    def line_up(peer):
        for pair in range(2):
            gathered[pl.ds(pair * peers + peer, 5, stride=2 * peers), :] = parcel_in[peer * 2 + pair]

    loop(peers, line_up, 8)
    low8, low4 = (lane8 & 15) < 8, (lane4 & 15) < 8
    for c in range(5):
        value = gathered[pl.ds(c * 2 * peers, 2 * peers), :]
        coarse_part = value.astype(jnp.bfloat16)
        rest = (value - coarse_part.astype(f32)).astype(jnp.bfloat16)
        sums = [contract(chosen[h], coarse_part) + contract(chosen[h], rest) for h in range(2)]
        change = {}
        for face in range(6):
            scale = 0.08 if face % 2 else -0.08
            for half in range(2):
                at = (face * 2 + half) * 8
                first, second = sums[0][at : at + 8], sums[1][at : at + 8]
                count = counts[at : at + 8]
                lows = first + pltpu.roll(second, 120, 1)
                highs = second + pltpu.roll(first, 8, 1)
                total = jnp.where(low4, lows[:4], highs[4:])
                number = jnp.where(low4, count[:4], count[4:])
                flux = flux_in[face, c, :, pl.ds(half * 128, 128)]
                change[face, half] = scale * (number * flux - total)
        stacked = {
            face: jnp.concatenate([change[face, 0], change[face, 1]], axis=0) for face in range(2, 6)
        }
        for x8 in range(8):
            for yh8 in range(2):
                shift = (112 * yh8 - 16 * x8) % 128
                moved = stacked[2 + yh8]
                moved = moved if shift == 0 else pltpu.roll(moved, shift, 1)
                added = jnp.where((lane8 >> 4) == 7 * yh8, moved, 0.0)
                index = x8 * 16 + 8 * yh8 + (lane8 >> 4)
                added = added + jnp.where((lane8 & 15) == 0, pick(stacked[4], index), 0.0)
                added = added + jnp.where((lane8 & 15) == 15, pick(stacked[5], index), 0.0)
                for upper in range(2):
                    x_at = 8 * upper + x8
                    at = pl.ds((2 * x_at + yh8) * 128, 128)
                    value = new_in[c, :, at] + added[4 * upper : 4 * upper + 4]
                    if x_at == 0:
                        value = value + change[0, yh8]
                    if x_at == 15:
                        value = value + change[1, yh8]
                    coarse_out[c, :, at] = value
        store = pltpu.make_async_copy(coarse_out.at[c], coarse_hand.at[c], store_sem.at[c])
        store.start()
        stores.append(store)
    for store in stores:
        store.wait()


def hand_over(fine, coarse, fine_out, coarse_out, fine_stage, coarse_stage, in_sem, out_sem):
    trips = []
    for c in range(5):
        for k, (source, stage, target) in enumerate(
            ((fine, fine_stage, fine_out), (coarse, coarse_stage, coarse_out))
        ):
            trips.append(
                (
                    pltpu.make_async_copy(source.at[c], stage.at[c], in_sem.at[2 * c + k]),
                    pltpu.make_async_copy(stage.at[c], target.at[c], out_sem.at[2 * c + k]),
                )
            )
    for arrive, _ in trips:
        arrive.start()
    for arrive, leave in trips:
        arrive.wait()
        leave.start()
    for _, leave in trips:
        leave.wait()


def on_device(sizes, fine_old, send_left, send_right, new_source, face_source, request_slot, request_code,
              coarse_old, coarse_new, coarse_flux):
    peers = sizes[1] * sizes[2]
    smem = pl.BlockSpec(memory_space=pltpu.SMEM)
    hbm = pl.BlockSpec(memory_space=pltpu.HBM)
    dma = pltpu.SemaphoreType.DMA
    V = pltpu.VMEM
    fine, coarse = pl.pallas_call(
        functools.partial(kernel, sizes),
        out_shape=(
            jax.ShapeDtypeStruct((5, SLOTS, 4096), f32),
            jax.ShapeDtypeStruct((5, CSLOTS, 4096), f32),
        ),
        in_specs=[smem] * 6 + [hbm] * 4,
        out_specs=(hbm, hbm),
        scratch_shapes=[
            V((5, SLOTS, 4096), f32),
            V((5, CSLOTS, 4096), f32),
            V((5, CSLOTS, 4096), f32),
            V((6, 5, CSLOTS, 256), f32),
            V((peers, 1, 128), i32),
            V((peers, 1, 128), i32),
            pltpu.SMEM((peers, 1, 128), i32),
            V((2, 1, 128), i32),
            V((2, 1, 128), i32),
            pltpu.SMEM((2, 1, 128), i32),
            pltpu.SMEM((FACES,), i32),
            pltpu.SMEM((8,), i32),
            pltpu.SMEM((peers * CAP,), i32),
            pltpu.SMEM((8,), i32),
            V((8 * 160, 128), f32),
            V((416, 128), f32),
            V((2816, 128), f32),
            V((SLOTS, 5, 32, 128), f32),
            V((12, 5, 32, 128), f32),
            V((2, 2, 5, 32, 128), f32),
            V((2, 2, 5, 32, 128), f32),
            V((224, 8, 128), f32),
            V((peers * CAP, 5, 128), f32),
            V((peers * CAP, 5, 128), f32),
            V((18, 5, 32, 128), f32),
            V((18, 5, 32, 128), f32),
            V((8 * 160, 128), f32),
            V((6, 8, 128), i32),
            V((6, 2, 32, 128), f32),
            V((3, 32, 128), i32),
            V((3, 32, 128), i32),
            V((2, 3, 10, 128), f32),
            V((2, 3, 10, 128), f32),
            V((2, 3, 10, 128), f32),
            V((2, 3, 10, 128), f32),
            V((5, 16, 128), f32),
            V((2, 5, 16, 128), f32),
            V((128, 128), f32),
            V((FACEREQ, 5, 128), f32),
            V((peers * 2, 5, 128), f32),
            V((peers * 2, 5, 128), f32),
            V((8 * 2 * peers, 128), f32),
            V((peers, 128), i32),
            V((5, SLOTS, 4096), f32),
            V((5, CSLOTS, 4096), f32),
            dma((6,)),
            dma((4,)),
            dma((2,)),
            dma((peers,)),
            dma((peers,)),
            dma((2,)),
            dma((2,)),
            dma((2,)),
            dma((2,)),
            dma((peers,)),
            dma((peers,)),
            dma((2, 2)),
            dma((2, 2)),
            dma((peers,)),
            dma((peers,)),
        ],
        compiler_params=pltpu.CompilerParams(
            collective_id=0, has_side_effects=True, vmem_limit_bytes=64 * 1024 * 1024
        ),
    )(
        send_left,
        send_right,
        new_source,
        face_source,
        request_slot,
        request_code,
        jnp.transpose(fine_old, (1, 0, 2)),
        jnp.transpose(coarse_old, (1, 0, 2)),
        jnp.transpose(coarse_new, (1, 0, 2)),
        jnp.transpose(coarse_flux, (1, 2, 0, 3)),
    )
    fine, coarse = pl.pallas_call(
        hand_over,
        out_shape=(
            jax.ShapeDtypeStruct((5, SLOTS, 4096), f32),
            jax.ShapeDtypeStruct((5, CSLOTS, 4096), f32),
        ),
        in_specs=[hbm, hbm],
        out_specs=(hbm, hbm),
        scratch_shapes=[
            V((5, SLOTS, 4096), f32),
            V((5, CSLOTS, 4096), f32),
            dma((10,)),
            dma((10,)),
        ],
        compiler_params=pltpu.CompilerParams(vmem_limit_bytes=64 * 1024 * 1024),
    )(fine, coarse)
    return jnp.transpose(fine, (1, 0, 2)), jnp.transpose(coarse, (1, 0, 2))


def solution(mesh):
    sizes = (mesh.shape["gx"], mesh.shape["gy"], mesh.shape["gz"])
    every = ("gx", "gy", "gz")
    in_specs = (
        P(every, None, None),
        P(every),
        P(every),
        P(every),
        P(every, None),
        P(every),
        P(every),
        P(every, None, None),
        P(every, None, None),
        P(every, None, None, None),
    )
    out_specs = (P(every, None, None), P(every, None, None))
    return jax.shard_map(
        functools.partial(on_device, sizes), mesh=mesh, in_specs=in_specs, out_specs=out_specs, check_vma=False
    )
```
